512 devices in a mesh: replica: 32 (over z_lo, x), tp: 16 (over z_hi, y, core).
Axes of the slice: x: 4, y: 4, z: 16 (z_hi: 2, z_lo: 8; z = z_hi * 8 + z_lo), core: 2. Of those that a mesh axis runs over, the one named last changes fastest.
Arguments:
- kv_cache: bfloat16 [128, 2, 2048, 1024], P('replica', None, 'tp')
- lengths: int32 [128], P('replica'), may hold values from 2 to 2048, as said below
- queries: bfloat16 [3, 128, 64, 128], P(None, 'replica')
- new_kv: bfloat16 [3, 128, 2, 1024], P(None, 'replica'), may hold values from -6 to 6
- moving_slot: int32 [32], P('replica'), may hold values from 0 to 3
- destination: int32 [32], replicated, may hold values from 0 to 31, as said below
- block_index: int32 [32], P('replica'), may hold values from 0 to 3
Outputs:
- attended: bfloat16 [3, 128, 64, 128], P(None, 'replica', 'tp')
- arrived: bfloat16 [32, 2, 512, 1024], P('replica', None, 'tp')
- handed: bfloat16 [32, 3, 2, 1024], P('replica')
The draws below stay inside these ranges and needn't reach their ends.
Inputs may be any that keep to these rules, and one draw needn't show every extreme that they name: `lengths`: the longest request fills its cache. `destination`: a permutation of the replicas without fixed points.
All inputs are finite; a program needn't handle non-finite values.
Results may differ from the reference program's by a relative error of at most 0.0065.
Values may be sent and summed in bfloat16 or wider, within the bound.
No kernel may reach another device: no remote copies, remote signals or barrier semaphores. Data moves between devices by JAX's collectives and lax.ppermute only.
A program may use at most 64 MiB of HBM per device.

```python
import math
import jax
import jax.numpy as jnp
from jax import lax

HEADS = 64
KVH = 8
HD = 128
REQ_DEV = 4
POS_DEV = 128
STEPS = 3
BLOCK = 32
REQUESTS = 128
LEN = 2048
N_REPLICA = 32
N_TP = 16


def anchor_rows(key):
    base = jax.random.normal(jax.random.fold_in(key, 11), (REQUESTS, 2, 2, KVH * HD), jnp.float32)
    spread = jnp.exp(jax.random.uniform(jax.random.fold_in(key, 12), (REQUESTS, 1, 2, 1), jnp.float32, -0.7, 0.7))
    return base * spread


def draw_kv_cache(key, part):
    shared = anchor_rows(key)
    key = jax.random.fold_in(key, 3)
    remainder = jax.random.normal(key, (REQUESTS, 2, LEN - 2, KVH * HD), jnp.float32)
    spread = jnp.exp(jax.random.uniform(jax.random.fold_in(key, 1), (REQUESTS, 1, LEN - 2, 1), jnp.float32, -0.7, 0.7))
    return jnp.concatenate([shared, remainder * spread], axis=2).astype(jnp.bfloat16)


def draw_queries(key, part):
    key = jax.random.fold_in(key, 5)
    base = jax.random.normal(key, (STEPS, REQUESTS, HEADS, HD), jnp.float32)
    return base.astype(jnp.bfloat16)


def draw_lengths(key, part):
    key = jax.random.fold_in(key, 7)
    drawn = jax.random.randint(key, (REQUESTS,), 2, LEN + 1)
    fullest = jax.random.randint(jax.random.fold_in(key, 1), (), 0, REQUESTS)
    return jnp.where(jnp.arange(REQUESTS) == fullest, LEN, drawn).astype(jnp.int32)


def draw_destination(key, part):
    key = jax.random.fold_in(key, 9)
    order = jax.random.permutation(key, N_REPLICA)
    return jnp.zeros((N_REPLICA,), jnp.int32).at[order].set(jnp.roll(order, -1)).astype(jnp.int32)


def with_ends(array, key, smallest, high):
    dims = array.shape
    spot = [jax.random.randint(jax.random.fold_in(key, axis), (), 0, dims[axis]) for axis in range(len(dims))]
    array = array.at[tuple(spot)].set(smallest)
    longest = dims.index(max(dims))
    spot[longest] = (spot[longest] + 1) % dims[longest]
    return array.at[tuple(spot)].set(high)


def block_scale(key, extent, pieces, low, top_value):
    loudness = 1.0
    for position, blocks in pieces:
        steps = jax.random.uniform(jax.random.fold_in(jax.random.fold_in(key, 6), position), (blocks,), jnp.float32, low / len(pieces), top_value / len(pieces))
        loudness = loudness * jnp.repeat(jnp.exp(steps), extent[position] // blocks).reshape((-1,) + (1,) * (len(extent) - 1 - position))
    return loudness


def noise(key, shape, scale, reach, cuts=(), kind=jnp.bfloat16):
    factor_of = block_scale(key, shape, cuts, -0.22, 0.18) if cuts else 1.0
    result = jax.random.normal(key, shape, jnp.float32) * scale * factor_of
    return jnp.minimum(jnp.maximum(result, -reach), reach).astype(kind)


def setup_inputs(seed: int = 0) -> dict:
    key_of = jax.random.split(jax.random.key(seed), 8)
    kv_cache = draw_kv_cache(jax.random.fold_in(key_of[7], 71), 0)
    lengths = draw_lengths(jax.random.fold_in(key_of[7], 71), 0)
    queries = draw_queries(jax.random.fold_in(key_of[7], 71), 0)
    new_kv = noise(key_of[3], (STEPS, REQUESTS, 2, KVH * HD), 1.0, 6.0, ((1, 32),))
    moving_slot = with_ends(jax.random.randint(key_of[4], (N_REPLICA,), 0, REQ_DEV), jax.random.fold_in(key_of[4], 1), 0, REQ_DEV - 1).astype(jnp.int32)
    destination = draw_destination(jax.random.fold_in(key_of[7], 71), 0)
    block_index = with_ends(jax.random.randint(key_of[6], (N_REPLICA,), 0, POS_DEV // BLOCK), jax.random.fold_in(key_of[6], 1), 0, (POS_DEV // BLOCK) - 1).astype(jnp.int32)
    return {"kv_cache": kv_cache, "lengths": lengths, "queries": queries, "new_kv": new_kv, "moving_slot": moving_slot, "destination": destination, "block_index": block_index}


def attend(cache, length, query, fresh):
    factor = 1.0 / math.sqrt(HD)
    group_size = HEADS // KVH
    cache_keys = cache[0].reshape(LEN, KVH, HD).astype(jnp.float32)
    cache_values = cache[1].reshape(LEN, KVH, HD).astype(jnp.float32)
    grouped = query.reshape(STEPS, KVH, group_size, HD).astype(jnp.float32)
    new_keys = fresh[:, 0].reshape(STEPS, KVH, HD).astype(jnp.float32)
    new_values = fresh[:, 1].reshape(STEPS, KVH, HD).astype(jnp.float32)
    old_scores = jnp.einsum('skgd,pkd->skgp', grouped, cache_keys) * factor
    new_scores = jnp.einsum('skgd,tkd->skgt', grouped, new_keys) * factor
    live = jnp.arange(LEN, dtype=jnp.int32) < length
    old_mask = jnp.broadcast_to(live[None, None, None, :], old_scores.shape)
    causal = jnp.arange(STEPS, dtype=jnp.int32)[None, :] <= jnp.arange(STEPS, dtype=jnp.int32)[:, None]
    new_mask = jnp.broadcast_to(causal[:, None, None, :], new_scores.shape)
    scores = jnp.concatenate([jnp.where(old_mask, old_scores, -1e+30), jnp.where(new_mask, new_scores, -1e+30)], axis=-1)
    visible = jnp.concatenate([old_mask, new_mask], axis=-1)
    row_max = lax.optimization_barrier(jnp.max(scores, axis=-1, keepdims=True))
    weights = jnp.where(visible, jnp.exp(scores - row_max), 0.0)
    total = lax.optimization_barrier(jnp.sum(weights, axis=-1))
    rounded = lax.optimization_barrier(weights.astype(jnp.bfloat16)).astype(jnp.float32)
    every_value = jnp.concatenate([cache_values, new_values], axis=0)
    summed = jnp.einsum('skgp,pkd->skgd', rounded, every_value)
    return (summed / total[..., None]).astype(jnp.bfloat16).reshape(STEPS, HEADS, HD)

def reference(kv_cache, lengths, queries, new_kv, moving_slot, destination, block_index):
    by_request = (kv_cache, lengths, jnp.moveaxis(queries, 1, 0), jnp.moveaxis(new_kv, 1, 0))
    attended = lax.map(lambda items: attend(items[0], items[1], items[2], items[3]), by_request)
    attended = jnp.moveaxis(attended, 0, 1)
    sources = jnp.zeros((N_REPLICA,), jnp.int32).at[destination].set(jnp.arange(N_REPLICA, dtype=jnp.int32))

    def collect(source):
        request = (source * REQ_DEV + moving_slot[source]).astype(jnp.int32)
        cache = lax.dynamic_index_in_dim(kv_cache, request, 0, keepdims=False)
        cache = cache.reshape(2, N_TP, POS_DEV, KVH * HD)
        start = (block_index[source] * BLOCK).astype(jnp.int32)
        block = lax.dynamic_slice_in_dim(cache, start, BLOCK, 2).reshape(2, N_TP * BLOCK, KVH * HD)
        tokens = lax.dynamic_index_in_dim(new_kv, request, 1, keepdims=False)
        return (block, tokens)
    arrived, handed = lax.map(collect, sources)
    return (attended, arrived, handed)
```

```python
import functools
import math

import jax
import jax.numpy as jnp
from jax import lax
from jax.experimental import pallas as pl
from jax.experimental.pallas import tpu as pltpu
from jax.sharding import PartitionSpec as P

BLOCK = 32
HALF = 16
SLOT = 40
LANES = 128
HIDDEN = -1e30


def pack_kernel(slot_ref, block_ref, cache_ref, token_ref, out_ref):
    row = lax.broadcasted_iota(jnp.int32, (8, LANES), 0)
    for pair in range(2):
        for tile in range(8):
            columns = pl.ds(tile * LANES, LANES)
            piece = cache_ref[0, pair, :, columns]
            tokens = jnp.zeros((8, LANES), jnp.float32)
            for step in range(3):
                line = token_ref[step, 0, :, columns].astype(jnp.float32)[pair : pair + 1]
                tokens = jnp.where(row == step, line, tokens)
            whole = jnp.concatenate([piece.astype(jnp.float32), tokens], axis=0).astype(jnp.bfloat16)
            for half in range(2):
                out_ref[half * HALF + pair * 8 + tile] = whole


def pack(kv_cache, new_kv, moving_slot, block_index):
    width = kv_cache.shape[-1]
    return pl.pallas_call(
        pack_kernel,
        grid_spec=pltpu.PrefetchScalarGridSpec(
            num_scalar_prefetch=2,
            grid=(1,),
            in_specs=[
                pl.BlockSpec((1, 2, BLOCK, width), lambda i, slot, block: (slot[0], 0, block[0], 0)),
                pl.BlockSpec((3, 1, 2, width), lambda i, slot, block: (0, slot[0], 0, 0)),
            ],
            out_specs=pl.BlockSpec((2 * HALF, SLOT, LANES), lambda i, slot, block: (0, 0, 0)),
        ),
        out_shape=jax.ShapeDtypeStruct((2 * HALF, SLOT, LANES), jnp.bfloat16),
        cost_estimate=pl.CostEstimate(flops=0, bytes_accessed=1 << 20, transcendentals=0),
        name="pack",
    )(moving_slot, block_index, kv_cache, new_kv)


def reorder_kernel(destination_ref, mine_ref, in_ref, out_ref, source_ref):
    for source in range(2 * HALF):
        source_ref[destination_ref[source]] = source
    base = mine_ref[0] // HALF * HALF
    for slot in range(HALF):
        out_ref[slot] = in_ref[source_ref[base + slot]]


def reorder(destination, mine, pieces):
    return pl.pallas_call(
        reorder_kernel,
        grid_spec=pltpu.PrefetchScalarGridSpec(
            num_scalar_prefetch=2,
            grid=(1,),
            in_specs=[pl.BlockSpec((2 * HALF, SLOT, LANES), lambda i, a, b: (0, 0, 0))],
            out_specs=pl.BlockSpec((HALF, SLOT, LANES), lambda i, a, b: (0, 0, 0)),
            scratch_shapes=[pltpu.SMEM((2 * HALF,), jnp.int32)],
        ),
        out_shape=jax.ShapeDtypeStruct((HALF, SLOT, LANES), jnp.bfloat16),
        cost_estimate=pl.CostEstimate(flops=0, bytes_accessed=1 << 20, transcendentals=0),
        name="reorder",
    )(destination, mine, pieces)


def unpack_kernel(in_ref, arrived_ref, handed_ref):
    row = lax.broadcasted_iota(jnp.int32, (2, LANES), 0)
    for tile in range(8):
        columns = pl.ds(tile * LANES, LANES)
        lines = []
        for pair in range(2):
            whole = in_ref[pair * 8 + tile].astype(jnp.float32)
            arrived_ref[0, pair, :, columns] = whole[:BLOCK].astype(jnp.bfloat16)
            lines.append(whole[BLOCK:])
        for step in range(3):
            both = jnp.where(row == 0, lines[0][step : step + 1], lines[1][step : step + 1])
            handed_ref[0, step, :, columns] = both.astype(jnp.bfloat16)


def unpack(pieces, width):
    return pl.pallas_call(
        unpack_kernel,
        in_specs=[pl.BlockSpec(memory_space=pltpu.VMEM)],
        out_specs=[pl.BlockSpec(memory_space=pltpu.VMEM)] * 2,
        out_shape=(
            jax.ShapeDtypeStruct((1, 2, BLOCK, width), jnp.bfloat16),
            jax.ShapeDtypeStruct((1, 3, 2, width), jnp.bfloat16),
        ),
        cost_estimate=pl.CostEstimate(flops=0, bytes_accessed=1 << 20, transcendentals=0),
        name="unpack",
    )(pieces)


def partial_kernel(lengths_ref, rank_ref, cache_ref, query_ref, out_ref):
    request = pl.program_id(0)
    factor = 1.0 / math.sqrt(LANES)
    pos_dev = cache_ref.shape[2]
    position = rank_ref[0] * pos_dev + lax.broadcasted_iota(jnp.int32, (32, pos_dev), 1)
    live = position < lengths_ref[request]
    row8 = lax.broadcasted_iota(jnp.int32, (8, LANES), 0)
    top = row8 < 4
    row = lax.broadcasted_iota(jnp.int32, (32, LANES), 0) % 16
    lane = lax.broadcasted_iota(jnp.int32, (32, LANES), 1)
    group = lane // 16
    diagonal = lane % 16 == row
    steps = [query_ref[step, 0].astype(jnp.float32) for step in range(3)]
    for head in range(8):
        q0, q1, q2 = (part[head * 8 : head * 8 + 8] for part in steps)
        rolled0, rolled1, rolled2 = (pltpu.roll(part, 4, 0) for part in (q0, q1, q2))
        zero = jnp.zeros_like(q0)
        query = jnp.concatenate(
            [
                jnp.where(top, q0, rolled1),
                jnp.where(top, q2, zero),
                jnp.where(top, rolled0, q1),
                jnp.where(top, rolled2, zero),
            ],
            axis=0,
        ).astype(jnp.bfloat16)
        columns = pl.ds(head * LANES, LANES)
        scores = lax.dot_general(
            query,
            cache_ref[0, 0, :, columns],
            (((1,), (1,)), ((), ())),
            preferred_element_type=jnp.float32,
        )
        scores = jnp.where(live, scores * factor, HIDDEN)
        top_score = jnp.max(scores, axis=1, keepdims=True)
        weights = jnp.where(live, jnp.exp(scores - top_score), 0.0)
        total = jnp.sum(weights, axis=1, keepdims=True)
        summed = jnp.dot(
            weights.astype(jnp.bfloat16),
            cache_ref[0, 1, :, columns],
            preferred_element_type=jnp.float32,
        )
        max_high = top_score.astype(jnp.bfloat16).astype(jnp.float32)
        rest = top_score - max_high
        max_mid = rest.astype(jnp.bfloat16).astype(jnp.float32)
        max_low = rest - max_mid
        total_high = total.astype(jnp.bfloat16).astype(jnp.float32)
        total_low = total - total_high
        stats = jnp.where(group == 0, max_high, 0.0)
        stats = jnp.where(group == 1, max_mid, stats)
        stats = jnp.where(group == 2, max_low, stats)
        stats = jnp.where(group == 3, total_high, stats)
        stats = jnp.where(group == 4, total_low, stats)
        stats = jnp.where(diagonal, stats, 0.0)
        for half in range(2):
            rows = slice(half * 16, half * 16 + 16)
            line = jnp.sum(stats[rows], axis=0, keepdims=True)
            chunk = jnp.where(row[rows] == 12, line, summed[rows])
            out_ref[2 * head + half, 0] = chunk.astype(jnp.bfloat16)


def partials(kv_cache, queries, lengths, rank):
    req_dev, pair, pos_dev, width = kv_cache.shape
    steps, _, heads, head_dim = queries.shape
    return pl.pallas_call(
        partial_kernel,
        grid_spec=pltpu.PrefetchScalarGridSpec(
            num_scalar_prefetch=2,
            grid=(req_dev,),
            in_specs=[
                pl.BlockSpec((1, pair, pos_dev, width), lambda r, a, b: (r, 0, 0, 0)),
                pl.BlockSpec((steps, 1, heads, head_dim), lambda r, a, b: (0, r, 0, 0)),
            ],
            out_specs=pl.BlockSpec((16, 1, 16, LANES), lambda r, a, b: (0, r, 0, 0)),
        ),
        out_shape=jax.ShapeDtypeStruct((16, req_dev, 16, LANES), jnp.bfloat16),
        cost_estimate=pl.CostEstimate(
            flops=4 * 32 * 8 * req_dev * pos_dev * head_dim,
            bytes_accessed=12 << 20,
            transcendentals=32 * 8 * req_dev * pos_dev,
        ),
        name="partials",
    )(lengths, rank, kv_cache, queries)


def merge_kernel(rank_ref, chunk_ref, query_ref, token_ref, out_ref):
    rank = rank_ref[0]
    kv_head = rank // 2
    factor = 1.0 / math.sqrt(LANES)
    sources = chunk_ref.shape[0]
    row = lax.broadcasted_iota(jnp.int32, (16, LANES), 0)
    lane = lax.broadcasted_iota(jnp.int32, (16, LANES), 1)
    diagonal = lane % 16 == row
    spread_group = lax.broadcasted_iota(jnp.int32, (LANES, 2 * LANES), 0) // 16
    spread_total = lax.broadcasted_iota(jnp.int32, (LANES, 2 * LANES), 1) >= LANES
    spread = jnp.where(
        spread_total,
        jnp.where((spread_group == 3) | (spread_group == 4), 1.0, 0.0),
        jnp.where(spread_group < 3, 1.0, 0.0),
    ).astype(jnp.bfloat16)
    row8 = lax.broadcasted_iota(jnp.int32, (8, LANES), 0)
    columns = pl.ds(pl.multiple_of(kv_head * LANES, LANES), LANES)
    for request in range(chunk_ref.shape[1]):
        chunks = [chunk_ref[source, request].astype(jnp.float32) for source in range(sources)]
        lines = [jnp.where(diagonal, chunk[12:13], 0.0) for chunk in chunks]
        stats = jnp.dot(
            jnp.concatenate(lines, axis=0).astype(jnp.bfloat16),
            spread,
            preferred_element_type=jnp.float32,
        )
        tops = [stats[16 * source : 16 * source + 16, :LANES] for source in range(sources)]
        totals = [stats[16 * source : 16 * source + 16, LANES:] for source in range(sources)]
        parts = []
        for step in range(3):
            pair = query_ref[step, request, pl.ds(pl.multiple_of(rank // 4 * 16, 16), 16), :]
            pair = pair.astype(jnp.float32)
            tile = jnp.where((rank // 2) % 2 == 1, pair[8:], pair[:8])
            parts.append(jnp.where(rank % 2 == 1, pltpu.roll(tile, 4, 0), tile))
        query = jnp.concatenate(
            [jnp.where(row8 < 4, parts[0], pltpu.roll(parts[1], 4, 0)), parts[2]], axis=0
        )
        scores, values = [], []
        for step in range(3):
            token = token_ref[step, request, :, columns].astype(jnp.float32)
            score = jnp.sum(query * token[0:1], axis=1, keepdims=True) * factor
            scores.append(jnp.where(row >= 4 * step, score, HIDDEN))
            values.append(token[1:2])
        joint = functools.reduce(jnp.maximum, tops + scores)
        total = jnp.zeros((16, LANES), jnp.float32)
        summed = jnp.zeros((16, LANES), jnp.float32)
        for source in range(sources):
            scale = jnp.exp(tops[source] - joint)
            total += totals[source] * scale
            summed += chunks[source] * scale
        for step in range(3):
            weight = jnp.where(row >= 4 * step, jnp.exp(scores[step] - joint), 0.0)
            total += weight
            summed += weight.astype(jnp.bfloat16).astype(jnp.float32) * values[step]
        attended = summed / total
        for step in range(3):
            out_ref[step, request] = attended[4 * step : 4 * step + 4].astype(jnp.bfloat16)


def merge(rank, chunks, queries, new_kv):
    steps, req_dev, _, head_dim = queries.shape
    return pl.pallas_call(
        merge_kernel,
        in_specs=[pl.BlockSpec(memory_space=pltpu.SMEM)] + [pl.BlockSpec(memory_space=pltpu.VMEM)] * 3,
        out_specs=pl.BlockSpec(memory_space=pltpu.VMEM),
        out_shape=jax.ShapeDtypeStruct((steps, req_dev, 4, head_dim), jnp.bfloat16),
        cost_estimate=pl.CostEstimate(flops=0, bytes_accessed=6 << 20, transcendentals=0),
        name="merge",
    )(rank, chunks, queries, new_kv)


def body(kv_cache, lengths, queries, new_kv, moving_slot, destination, block_index):
    rank = lax.axis_index("tp").astype(jnp.int32)[None]
    mine = lax.axis_index("replica").astype(jnp.int32)[None]
    sent = pack(kv_cache, new_kv, moving_slot, block_index)
    pieces = lax.all_to_all(sent, "replica", 0, 0, tiled=True)
    local = partials(kv_cache, queries, lengths, rank)
    chunks = lax.all_to_all(local, "tp", 0, 0, tiled=True)
    ordered = reorder(destination, mine, pieces)
    halves = [list(range(HALF)), list(range(HALF, 2 * HALF))]
    delivered = lax.all_to_all(ordered, "replica", 0, 0, tiled=True, axis_index_groups=halves)
    attended = merge(rank, chunks, queries, new_kv)
    arrived, handed = unpack(delivered, kv_cache.shape[-1])
    return (attended, arrived, handed)


def solution(mesh):
    placed = (
        P("replica", None, "tp", None),
        P("replica"),
        P(None, "replica", None, None),
        P(None, "replica", None, None),
        P("replica"),
        P(),
        P("replica"),
    )
    return jax.shard_map(
        body,
        mesh=mesh,
        in_specs=placed,
        out_specs=(
            P(None, "replica", "tp", None),
            P("replica", None, "tp", None),
            P("replica", None, None, None),
        ),
        check_vma=False,
    )
```

```python
import functools
import math

import jax
import jax.numpy as jnp
from jax import lax
from jax.experimental import pallas as pl
from jax.experimental.pallas import tpu as pltpu
from jax.sharding import PartitionSpec as P

BLOCK = 32
HALF = 16
SLOT = 40
CHUNK = 56
LANES = 128
HIDDEN = -1e30
FACTOR = 1.0 / math.sqrt(LANES)
LIMIT = 16 << 20
FRONT_LIMIT = 61 << 20


def front_kernel(
    place_ref, lengths_hbm, cache_hbm, query_hbm, local_ref,
    lengths_ref, cache_ref, query_ref, lengths_sem, cache_sem, query_sem,
):
    requests, _, pos_dev, _ = cache_ref.shape
    lengths_copy = pltpu.make_async_copy(lengths_hbm, lengths_ref, lengths_sem)
    lengths_copy.start()
    query_copy = pltpu.make_async_copy(query_hbm, query_ref, query_sem)
    query_copy.start()
    cache_copies = [
        pltpu.make_async_copy(cache_hbm.at[r], cache_ref.at[r], cache_sem.at[r]) for r in range(requests)
    ]
    for copy in cache_copies:
        copy.start()

    position = place_ref[0] * pos_dev + lax.broadcasted_iota(jnp.int32, (8, pos_dev), 1)
    lane = lax.broadcasted_iota(jnp.int32, (8, LANES), 1)
    top = lax.broadcasted_iota(jnp.int32, (8, LANES), 0) < 4
    lengths_copy.wait()
    query_copy.wait()

    def attend(r):
        live = position < lengths_ref[r]
        steps = [query_ref[step, r].astype(jnp.float32) for step in range(3)]
        scores = []
        for head in range(8):
            query = jnp.concatenate([part[head * 8 : head * 8 + 8] for part in steps], axis=0)
            scores.append(
                lax.dot_general(
                    query.astype(jnp.bfloat16),
                    cache_ref[r, 0, :, head * LANES : (head + 1) * LANES],
                    (((1,), (1,)), ((), ())),
                    preferred_element_type=jnp.float32,
                )
            )
        results = []
        for head in range(8):
            tiles, stats = [], []
            for step in range(3):
                score = jnp.where(live, scores[head][8 * step : 8 * step + 8] * FACTOR, HIDDEN)
                peak = jnp.max(score, axis=1, keepdims=True)
                weight = jnp.where(live, jnp.exp(score - peak), 0.0)
                total = jnp.sum(weight, axis=1, keepdims=True)
                tiles.append(weight)
                peak_high = peak.astype(jnp.bfloat16).astype(jnp.float32)
                rest = peak - peak_high
                peak_mid = rest.astype(jnp.bfloat16).astype(jnp.float32)
                total_high = total.astype(jnp.bfloat16).astype(jnp.float32)
                stats.append((peak_high, peak_mid, rest - peak_mid, total_high, total - total_high))
            summed = jnp.dot(
                jnp.concatenate(tiles, axis=0).astype(jnp.bfloat16),
                cache_ref[r, 1, :, head * LANES : (head + 1) * LANES],
                preferred_element_type=jnp.float32,
            )
            results.append((summed, stats))
        return results

    for pair in range(2):
        both = []
        for r in (2 * pair, 2 * pair + 1):
            cache_copies[r].wait()
            both.append(attend(r))
        for head in range(8):
            (sum_a, stats_a), (sum_b, stats_b) = both[0][head], both[1][head]
            table_a = jnp.zeros((8, LANES), jnp.float32)
            table_b = jnp.zeros((8, LANES), jnp.float32)
            for step in range(3):
                a, b = sum_a[8 * step : 8 * step + 8], sum_b[8 * step : 8 * step + 8]
                rows = slice(16 * step + 8 * pair, 16 * step + 8 * pair + 8)
                here = (2 * head % 8, head // 4, rows)
                local_ref[here] = jnp.where(top, a, pltpu.roll(b, 4, 0)).astype(jnp.bfloat16)
                here = (2 * head % 8 + 1, head // 4, rows)
                local_ref[here] = jnp.where(top, pltpu.roll(a, 4, 0), b).astype(jnp.bfloat16)
                for term in range(5):
                    here = lane == (step * 2 + pair) * 8 + term
                    table_a = jnp.where(here, stats_a[step][term], table_a)
                    table_b = jnp.where(here, stats_b[step][term], table_b)
            for half, table in (
                (0, jnp.where(top, table_a, pltpu.roll(table_b, 4, 0))),
                (1, jnp.where(top, pltpu.roll(table_a, 4, 0), table_b)),
            ):
                here = (2 * head % 8 + half, head // 4, slice(48, CHUNK))
                if pair == 1:
                    table = table + local_ref[here].astype(jnp.float32)
                local_ref[here] = table.astype(jnp.bfloat16)


def front(place, lengths, kv_cache, queries):
    req_dev = kv_cache.shape[0]
    return pl.pallas_call(
        front_kernel,
        in_specs=[pl.BlockSpec(memory_space=pltpu.SMEM)] + [pl.BlockSpec(memory_space=pl.ANY)] * 3,
        out_specs=pl.BlockSpec(memory_space=pltpu.VMEM),
        out_shape=jax.ShapeDtypeStruct((8, 2, CHUNK, LANES), jnp.bfloat16),
        scratch_shapes=[
            pltpu.SMEM(lengths.shape, jnp.int32),
            pltpu.VMEM(kv_cache.shape, jnp.bfloat16),
            pltpu.VMEM(queries.shape, jnp.bfloat16),
            pltpu.SemaphoreType.DMA(()),
            pltpu.SemaphoreType.DMA((req_dev,)),
            pltpu.SemaphoreType.DMA(()),
        ],
        compiler_params=pltpu.CompilerParams(vmem_limit_bytes=FRONT_LIMIT),
        name="front",
    )(place, lengths, kv_cache, queries)


def spread_of(index):
    term = lax.broadcasted_iota(jnp.int32, (LANES, 2 * LANES), 0) - index * 8
    second = lax.broadcasted_iota(jnp.int32, (LANES, 2 * LANES), 1) >= LANES
    maxima = jnp.where((term >= 0) & (term < 3), 1.0, 0.0)
    totals = jnp.where((term == 3) | (term == 4), 1.0, 0.0)
    return jnp.where(second, totals, maxima).astype(jnp.bfloat16)


def fold_kernel(
    place_ref, chunk_ref, cache_hbm, token_hbm, sent_ref, out_ref, moving_ref, token_ref, moving_sem, token_sem
):
    slot = place_ref[2]
    first = pl.multiple_of(place_ref[3] * BLOCK, BLOCK)
    moving_copy = pltpu.make_async_copy(cache_hbm.at[slot, :, pl.ds(first, BLOCK)], moving_ref, moving_sem)
    moving_copy.start()
    token_copy = pltpu.make_async_copy(token_hbm, token_ref, token_sem)
    token_copy.start()
    other = 1 - place_ref[0] // 8
    sources = chunk_ref.shape[0]
    lane = lax.broadcasted_iota(jnp.int32, (8, LANES), 1)
    tables = jnp.concatenate(
        [chunk_ref[source, other, 48:CHUNK].astype(jnp.float32) for source in range(sources)], axis=0
    ).astype(jnp.bfloat16)
    joined = jnp.zeros((8, LANES), jnp.float32)
    for index in range(6):
        stats = jnp.dot(tables, spread_of(index), preferred_element_type=jnp.float32)
        peaks = [stats[8 * source : 8 * source + 8, :LANES] for source in range(sources)]
        totals = [stats[8 * source : 8 * source + 8, LANES:] for source in range(sources)]
        joint = functools.reduce(jnp.maximum, peaks)
        total = jnp.zeros((8, LANES), jnp.float32)
        summed = jnp.zeros((8, LANES), jnp.float32)
        for source in range(sources):
            scale = jnp.exp(peaks[source] - joint)
            total += totals[source] * scale
            part = chunk_ref[source, other, 8 * index : 8 * index + 8]
            summed += part.astype(jnp.float32) * scale
        out_ref[8 * index : 8 * index + 8] = summed.astype(jnp.bfloat16)
        joint_high = joint.astype(jnp.bfloat16).astype(jnp.float32)
        rest = joint - joint_high
        joint_mid = rest.astype(jnp.bfloat16).astype(jnp.float32)
        total_high = total.astype(jnp.bfloat16).astype(jnp.float32)
        terms = (joint_high, joint_mid, rest - joint_mid, total_high, total - total_high)
        for term, value in enumerate(terms):
            joined = jnp.where(lane == index * 8 + term, value, joined)
    out_ref[48:CHUNK] = joined.astype(jnp.bfloat16)

    token_copy.wait()
    moving_copy.wait()
    row = lax.broadcasted_iota(jnp.int32, (8, LANES), 0)
    lines = [token_ref[step, slot].astype(jnp.float32) for step in range(3)]
    for kind in range(2):
        for tile in range(8):
            columns = slice(tile * LANES, (tile + 1) * LANES)
            tokens = jnp.zeros((8, LANES), jnp.float32)
            for step in range(3):
                tokens = jnp.where(row == step, lines[step][kind : kind + 1, columns], tokens)
            piece, tokens = moving_ref[kind, :, columns], tokens.astype(jnp.bfloat16)
            for half in range(2):
                sent_ref[half * HALF + kind * 8 + tile, :BLOCK] = piece
                sent_ref[half * HALF + kind * 8 + tile, BLOCK:] = tokens


def fold(place, chunks, kv_cache, new_kv):
    return pl.pallas_call(
        fold_kernel,
        in_specs=[
            pl.BlockSpec(memory_space=pltpu.SMEM),
            pl.BlockSpec(memory_space=pltpu.VMEM),
            pl.BlockSpec(memory_space=pl.ANY),
            pl.BlockSpec(memory_space=pl.ANY),
        ],
        out_specs=[pl.BlockSpec(memory_space=pltpu.VMEM)] * 2,
        out_shape=(
            jax.ShapeDtypeStruct((2 * HALF, SLOT, LANES), jnp.bfloat16),
            jax.ShapeDtypeStruct((CHUNK, LANES), jnp.bfloat16),
        ),
        scratch_shapes=[
            pltpu.VMEM((2, BLOCK, kv_cache.shape[-1]), jnp.bfloat16),
            pltpu.VMEM(new_kv.shape, jnp.bfloat16),
            pltpu.SemaphoreType.DMA(()),
            pltpu.SemaphoreType.DMA(()),
        ],
        compiler_params=pltpu.CompilerParams(vmem_limit_bytes=LIMIT),
        name="fold",
    )(place, chunks, kv_cache, new_kv)


def reorder_kernel(place_ref, destination_ref, in_ref, after_ref, out_ref, source_ref):
    del after_ref
    for source in range(2 * HALF):
        source_ref[destination_ref[source]] = source
    base = place_ref[1] // HALF * HALF
    for slot in range(HALF):
        out_ref[slot] = in_ref[source_ref[base + slot]]


def reorder(place, destination, pieces, after):
    return pl.pallas_call(
        reorder_kernel,
        in_specs=[pl.BlockSpec(memory_space=pltpu.SMEM)] * 2
        + [pl.BlockSpec(memory_space=pltpu.VMEM), pl.BlockSpec(memory_space=pl.ANY)],
        out_specs=pl.BlockSpec(memory_space=pltpu.VMEM),
        out_shape=jax.ShapeDtypeStruct((HALF, SLOT, LANES), jnp.bfloat16),
        scratch_shapes=[pltpu.SMEM((2 * HALF,), jnp.int32)],
        compiler_params=pltpu.CompilerParams(vmem_limit_bytes=LIMIT),
        name="reorder",
    )(place, destination, pieces, after)


def back_kernel(place_ref, piece_ref, chunk_ref, folded_ref, query_ref, token_ref, attended_ref, arrived_ref, handed_ref):
    row2 = lax.broadcasted_iota(jnp.int32, (2, LANES), 0)
    for tile in range(8):
        columns = slice(tile * LANES, (tile + 1) * LANES)
        lines = []
        for kind in range(2):
            arrived_ref[0, kind, :, columns] = piece_ref[kind * 8 + tile, :BLOCK]
            lines.append(piece_ref[kind * 8 + tile, BLOCK:].astype(jnp.float32))
        for step in range(3):
            both = jnp.where(row2 == 0, lines[0][step : step + 1], lines[1][step : step + 1])
            handed_ref[0, step, :, columns] = both.astype(jnp.bfloat16)

    rank = place_ref[0]
    sources = chunk_ref.shape[0]
    plane = rank // 8
    columns = pl.ds(pl.multiple_of(rank // 2 * LANES, LANES), LANES)
    top = lax.broadcasted_iota(jnp.int32, (8, LANES), 0) < 4
    tables = [chunk_ref[source, plane, 48:CHUNK].astype(jnp.float32) for source in range(sources)]
    tables.append(folded_ref[48:CHUNK].astype(jnp.float32))
    tables.append(jnp.zeros_like(tables[0]))
    tables = jnp.concatenate(tables, axis=0).astype(jnp.bfloat16)
    for pair in range(2):
        fresh_keys, fresh_values = [], []
        for token in range(3):
            a = token_ref[token, 2 * pair, :, columns].astype(jnp.float32)
            b = token_ref[token, 2 * pair + 1, :, columns].astype(jnp.float32)
            fresh_keys.append(jnp.where(top, a[0:1], b[0:1]))
            fresh_values.append(jnp.where(top, a[1:2], b[1:2]))
        for step in range(3):
            own = []
            for r in (2 * pair, 2 * pair + 1):
                wide = query_ref[step, r, pl.ds(pl.multiple_of(rank // 4 * 16, 16), 16), :].astype(jnp.float32)
                own.append(jnp.where(rank // 2 % 2 == 1, wide[8:], wide[:8]))
            a, b = own
            query = jnp.where(
                rank % 2 == 1,
                jnp.where(top, pltpu.roll(a, 4, 0), b),
                jnp.where(top, a, pltpu.roll(b, 4, 0)),
            )
            index = step * 2 + pair
            stats = jnp.dot(tables, spread_of(index), preferred_element_type=jnp.float32)
            peaks = [stats[8 * source : 8 * source + 8, :LANES] for source in range(sources + 1)]
            totals = [stats[8 * source : 8 * source + 8, LANES:] for source in range(sources + 1)]
            parts = [chunk_ref[source, plane, 8 * index : 8 * index + 8] for source in range(sources)]
            parts.append(folded_ref[8 * index : 8 * index + 8])
            scores = [
                jnp.sum(query * fresh_keys[token], axis=1, keepdims=True) * FACTOR for token in range(step + 1)
            ]
            joint = functools.reduce(jnp.maximum, peaks + scores)
            total = jnp.zeros((8, LANES), jnp.float32)
            summed = jnp.zeros((8, LANES), jnp.float32)
            for peak, share, part in zip(peaks, totals, parts, strict=True):
                scale = jnp.exp(peak - joint)
                total += share * scale
                summed += part.astype(jnp.float32) * scale
            for token in range(step + 1):
                weight = jnp.exp(scores[token] - joint)
                total += weight
                summed += weight.astype(jnp.bfloat16).astype(jnp.float32) * fresh_values[token]
            attended = summed / total
            attended_ref[step, 2 * pair] = attended[:4].astype(jnp.bfloat16)
            attended_ref[step, 2 * pair + 1] = attended[4:].astype(jnp.bfloat16)


def back(place, pieces, chunks, folded, queries, new_kv):
    steps, req_dev, _, head_dim = queries.shape
    width = new_kv.shape[-1]
    return pl.pallas_call(
        back_kernel,
        in_specs=[pl.BlockSpec(memory_space=pltpu.SMEM)] + [pl.BlockSpec(memory_space=pltpu.VMEM)] * 5,
        out_specs=[pl.BlockSpec(memory_space=pltpu.VMEM)] * 3,
        out_shape=(
            jax.ShapeDtypeStruct((steps, req_dev, 4, head_dim), jnp.bfloat16),
            jax.ShapeDtypeStruct((1, 2, BLOCK, width), jnp.bfloat16),
            jax.ShapeDtypeStruct((1, steps, 2, width), jnp.bfloat16),
        ),
        compiler_params=pltpu.CompilerParams(vmem_limit_bytes=LIMIT),
        name="back",
    )(place, pieces, chunks, folded, queries, new_kv)


def body(kv_cache, lengths, queries, new_kv, moving_slot, destination, block_index):
    place = jnp.stack([lax.axis_index("tp"), lax.axis_index("replica"), moving_slot[0], block_index[0]])
    place = place.astype(jnp.int32)
    local = front(place, lengths, kv_cache, queries)
    planes = [list(range(8)), list(range(8, 16))]
    chunks = lax.all_to_all(local, "tp", 0, 0, tiled=True, axis_index_groups=planes)
    sent, half_sum = fold(place, chunks, kv_cache, new_kv)
    folded = lax.ppermute(half_sum, "tp", [(i, i ^ 8) for i in range(16)])
    pieces = lax.all_to_all(sent, "replica", 0, 0, tiled=True)
    ordered = reorder(place, destination, pieces, folded)
    halves = [list(range(HALF)), list(range(HALF, 2 * HALF))]
    delivered = lax.all_to_all(ordered, "replica", 0, 0, tiled=True, axis_index_groups=halves)
    return back(place, delivered, chunks, folded, queries, new_kv)


def solution(mesh):
    placed = (
        P("replica", None, "tp", None),
        P("replica"),
        P(None, "replica", None, None),
        P(None, "replica", None, None),
        P("replica"),
        P(),
        P("replica"),
    )
    return jax.shard_map(
        body,
        mesh=mesh,
        in_specs=placed,
        out_specs=(
            P(None, "replica", "tp", None),
            P("replica", None, "tp", None),
            P("replica", None, None, None),
        ),
        check_vma=False,
    )
```

```python
import functools
import math

import jax
import jax.numpy as jnp
from jax import lax
from jax.experimental import pallas as pl
from jax.experimental.pallas import tpu as pltpu
from jax.sharding import PartitionSpec as P

BLOCK = 32
HALF = 16
SLOT = 40
CHUNK = 56
LANES = 128
HIDDEN = -1e30
FACTOR = 1.0 / math.sqrt(LANES)
LIMIT = 16 << 20
FRONT_LIMIT = 61 << 20


def pack_kernel(slot_ref, block_ref, cache_hbm, token_hbm, sent_ref, moving_ref, token_ref, moving_sem, token_sem):
    slot = slot_ref[0]
    first = pl.multiple_of(block_ref[0] * BLOCK, BLOCK)
    moving_copy = pltpu.make_async_copy(cache_hbm.at[slot, :, pl.ds(first, BLOCK)], moving_ref, moving_sem)
    moving_copy.start()
    token_copy = pltpu.make_async_copy(token_hbm, token_ref, token_sem)
    token_copy.start()
    row = lax.broadcasted_iota(jnp.int32, (8, LANES), 0)
    token_copy.wait()
    lines = [token_ref[step, slot].astype(jnp.float32) for step in range(3)]
    moving_copy.wait()
    for kind in range(2):
        for tile in range(8):
            columns = slice(tile * LANES, (tile + 1) * LANES)
            tokens = jnp.zeros((8, LANES), jnp.float32)
            for step in range(3):
                tokens = jnp.where(row == step, lines[step][kind : kind + 1, columns], tokens)
            sent_ref[kind * 8 + tile, :BLOCK] = moving_ref[kind, :, columns]
            sent_ref[kind * 8 + tile, BLOCK:] = tokens.astype(jnp.bfloat16)


def pack(moving_slot, block_index, kv_cache, new_kv):
    return pl.pallas_call(
        pack_kernel,
        in_specs=[
            pl.BlockSpec(memory_space=pltpu.SMEM),
            pl.BlockSpec(memory_space=pltpu.SMEM),
            pl.BlockSpec(memory_space=pl.ANY),
            pl.BlockSpec(memory_space=pl.ANY),
        ],
        out_specs=pl.BlockSpec(memory_space=pltpu.VMEM),
        out_shape=jax.ShapeDtypeStruct((HALF, SLOT, LANES), jnp.bfloat16),
        scratch_shapes=[
            pltpu.VMEM((2, BLOCK, kv_cache.shape[-1]), jnp.bfloat16),
            pltpu.VMEM(new_kv.shape, jnp.bfloat16),
            pltpu.SemaphoreType.DMA(()),
            pltpu.SemaphoreType.DMA(()),
        ],
        compiler_params=pltpu.CompilerParams(vmem_limit_bytes=FRONT_LIMIT),
        name="pack",
    )(moving_slot, block_index, kv_cache, new_kv)


def front_kernel(
    lengths_hbm, cache_hbm, query_hbm, after_ref, local_ref,
    lengths_ref, cache_ref, query_ref, lengths_sem, cache_sem, query_sem,
):
    del after_ref
    requests, _, pos_dev, _ = cache_ref.shape
    lengths_copy = pltpu.make_async_copy(lengths_hbm, lengths_ref, lengths_sem)
    lengths_copy.start()
    query_copy = pltpu.make_async_copy(query_hbm, query_ref, query_sem)
    query_copy.start()
    cache_copies = [
        pltpu.make_async_copy(cache_hbm.at[r], cache_ref.at[r], cache_sem.at[r]) for r in range(requests)
    ]
    for copy in cache_copies:
        copy.start()

    position = lax.axis_index("tp") * pos_dev + lax.broadcasted_iota(jnp.int32, (8, pos_dev), 1)
    lane = lax.broadcasted_iota(jnp.int32, (8, LANES), 1)
    top = lax.broadcasted_iota(jnp.int32, (8, LANES), 0) < 4
    lengths_copy.wait()
    query_copy.wait()

    def attend(r):
        live = position < lengths_ref[r]
        steps = [query_ref[step, r].astype(jnp.float32) for step in range(3)]
        scores = []
        for head in range(8):
            query = jnp.concatenate([part[head * 8 : head * 8 + 8] for part in steps], axis=0)
            scores.append(
                lax.dot_general(
                    query.astype(jnp.bfloat16),
                    cache_ref[r, 0, :, head * LANES : (head + 1) * LANES],
                    (((1,), (1,)), ((), ())),
                    preferred_element_type=jnp.float32,
                )
            )
        results = []
        for head in range(8):
            tiles, stats = [], []
            for step in range(3):
                score = jnp.where(live, scores[head][8 * step : 8 * step + 8] * FACTOR, HIDDEN)
                peak = jnp.max(score, axis=1, keepdims=True)
                weight = jnp.where(live, jnp.exp(score - peak), 0.0)
                total = jnp.sum(weight, axis=1, keepdims=True)
                tiles.append(weight)
                peak_high = peak.astype(jnp.bfloat16).astype(jnp.float32)
                rest = peak - peak_high
                peak_mid = rest.astype(jnp.bfloat16).astype(jnp.float32)
                total_high = total.astype(jnp.bfloat16).astype(jnp.float32)
                stats.append((peak_high, peak_mid, rest - peak_mid, total_high, total - total_high))
            summed = jnp.dot(
                jnp.concatenate(tiles, axis=0).astype(jnp.bfloat16),
                cache_ref[r, 1, :, head * LANES : (head + 1) * LANES],
                preferred_element_type=jnp.float32,
            )
            results.append((summed, stats))
        return results

    for pair in range(2):
        both = []
        for r in (2 * pair, 2 * pair + 1):
            cache_copies[r].wait()
            both.append(attend(r))
        for head in range(8):
            (sum_a, stats_a), (sum_b, stats_b) = both[0][head], both[1][head]
            table_a = jnp.zeros((8, LANES), jnp.float32)
            table_b = jnp.zeros((8, LANES), jnp.float32)
            for step in range(3):
                a, b = sum_a[8 * step : 8 * step + 8], sum_b[8 * step : 8 * step + 8]
                rows = slice(16 * step + 8 * pair, 16 * step + 8 * pair + 8)
                here = (2 * head % 8, head // 4, rows)
                local_ref[here] = jnp.where(top, a, pltpu.roll(b, 4, 0)).astype(jnp.bfloat16)
                here = (2 * head % 8 + 1, head // 4, rows)
                local_ref[here] = jnp.where(top, pltpu.roll(a, 4, 0), b).astype(jnp.bfloat16)
                for term in range(5):
                    here = lane == (step * 2 + pair) * 8 + term
                    table_a = jnp.where(here, stats_a[step][term], table_a)
                    table_b = jnp.where(here, stats_b[step][term], table_b)
            for half, table in (
                (0, jnp.where(top, table_a, pltpu.roll(table_b, 4, 0))),
                (1, jnp.where(top, pltpu.roll(table_a, 4, 0), table_b)),
            ):
                here = (2 * head % 8 + half, head // 4, slice(48, CHUNK))
                if pair == 1:
                    table = table + local_ref[here].astype(jnp.float32)
                local_ref[here] = table.astype(jnp.bfloat16)


def front(lengths, kv_cache, queries, after):
    req_dev = kv_cache.shape[0]
    return pl.pallas_call(
        front_kernel,
        in_specs=[pl.BlockSpec(memory_space=pl.ANY)] * 4,
        out_specs=pl.BlockSpec(memory_space=pltpu.VMEM),
        out_shape=jax.ShapeDtypeStruct((8, 2, CHUNK, LANES), jnp.bfloat16),
        scratch_shapes=[
            pltpu.SMEM(lengths.shape, jnp.int32),
            pltpu.VMEM(kv_cache.shape, jnp.bfloat16),
            pltpu.VMEM(queries.shape, jnp.bfloat16),
            pltpu.SemaphoreType.DMA(()),
            pltpu.SemaphoreType.DMA((req_dev,)),
            pltpu.SemaphoreType.DMA(()),
        ],
        compiler_params=pltpu.CompilerParams(vmem_limit_bytes=FRONT_LIMIT),
        name="front",
    )(lengths, kv_cache, queries, after)


def spread_of(index):
    term = lax.broadcasted_iota(jnp.int32, (LANES, 2 * LANES), 0) - index * 8
    second = lax.broadcasted_iota(jnp.int32, (LANES, 2 * LANES), 1) >= LANES
    maxima = jnp.where((term >= 0) & (term < 3), 1.0, 0.0)
    totals = jnp.where((term == 3) | (term == 4), 1.0, 0.0)
    return jnp.where(second, totals, maxima).astype(jnp.bfloat16)


def fold_kernel(destination_ref, chunk_ref, piece_ref, slot_ref, out_ref, source_ref):
    for source in range(2 * HALF):
        source_ref[destination_ref[source]] = source
    for target in range(2 * HALF):
        slot_ref[target] = piece_ref[source_ref[target] % HALF]
    other = 1 - lax.axis_index("tp") // 8
    sources = chunk_ref.shape[0]
    lane = lax.broadcasted_iota(jnp.int32, (8, LANES), 1)
    tables = jnp.concatenate(
        [chunk_ref[source, other, 48:CHUNK].astype(jnp.float32) for source in range(sources)], axis=0
    ).astype(jnp.bfloat16)
    joined = jnp.zeros((8, LANES), jnp.float32)
    for index in range(6):
        stats = jnp.dot(tables, spread_of(index), preferred_element_type=jnp.float32)
        peaks = [stats[8 * source : 8 * source + 8, :LANES] for source in range(sources)]
        totals = [stats[8 * source : 8 * source + 8, LANES:] for source in range(sources)]
        joint = functools.reduce(jnp.maximum, peaks)
        total = jnp.zeros((8, LANES), jnp.float32)
        summed = jnp.zeros((8, LANES), jnp.float32)
        for source in range(sources):
            scale = jnp.exp(peaks[source] - joint)
            total += totals[source] * scale
            part = chunk_ref[source, other, 8 * index : 8 * index + 8]
            summed += part.astype(jnp.float32) * scale
        out_ref[8 * index : 8 * index + 8] = summed.astype(jnp.bfloat16)
        joint_high = joint.astype(jnp.bfloat16).astype(jnp.float32)
        rest = joint - joint_high
        joint_mid = rest.astype(jnp.bfloat16).astype(jnp.float32)
        total_high = total.astype(jnp.bfloat16).astype(jnp.float32)
        terms = (joint_high, joint_mid, rest - joint_mid, total_high, total - total_high)
        for term, value in enumerate(terms):
            joined = jnp.where(lane == index * 8 + term, value, joined)
    out_ref[48:CHUNK] = joined.astype(jnp.bfloat16)


def fold(destination, chunks, pieces):
    return pl.pallas_call(
        fold_kernel,
        in_specs=[pl.BlockSpec(memory_space=pltpu.SMEM)] + [pl.BlockSpec(memory_space=pltpu.VMEM)] * 2,
        out_specs=[pl.BlockSpec(memory_space=pltpu.VMEM)] * 2,
        out_shape=(
            jax.ShapeDtypeStruct((2 * HALF, SLOT, LANES), jnp.bfloat16),
            jax.ShapeDtypeStruct((CHUNK, LANES), jnp.bfloat16),
        ),
        scratch_shapes=[pltpu.SMEM((2 * HALF,), jnp.int32)],
        compiler_params=pltpu.CompilerParams(vmem_limit_bytes=LIMIT),
        name="fold",
    )(destination, chunks, pieces)


def unpack_kernel(destination_ref, piece_ref, arrived_ref, handed_ref):
    mine = lax.axis_index("replica")
    origin = jnp.int32(0)
    for source in range(2 * HALF):
        origin = jnp.where(destination_ref[source] == mine, source // HALF * HALF, origin)
    row = lax.broadcasted_iota(jnp.int32, (2, LANES), 0)
    for tile in range(8):
        columns = slice(tile * LANES, (tile + 1) * LANES)
        lines = []
        for kind in range(2):
            arrived_ref[0, kind, :, columns] = piece_ref[origin + kind * 8 + tile, :BLOCK]
            lines.append(piece_ref[origin + kind * 8 + tile, BLOCK:].astype(jnp.float32))
        for step in range(3):
            both = jnp.where(row == 0, lines[0][step : step + 1], lines[1][step : step + 1])
            handed_ref[0, step, :, columns] = both.astype(jnp.bfloat16)


def unpack(destination, pieces, width):
    return pl.pallas_call(
        unpack_kernel,
        in_specs=[pl.BlockSpec(memory_space=pltpu.SMEM), pl.BlockSpec(memory_space=pltpu.VMEM)],
        out_specs=[pl.BlockSpec(memory_space=pltpu.VMEM)] * 2,
        out_shape=(
            jax.ShapeDtypeStruct((1, 2, BLOCK, width), jnp.bfloat16),
            jax.ShapeDtypeStruct((1, 3, 2, width), jnp.bfloat16),
        ),
        compiler_params=pltpu.CompilerParams(vmem_limit_bytes=LIMIT),
        name="unpack",
    )(destination, pieces)


def merge_kernel(chunk_ref, folded_ref, query_ref, token_ref, attended_ref):
    rank = lax.axis_index("tp")
    sources = chunk_ref.shape[0]
    plane = rank // 8
    columns = pl.ds(pl.multiple_of(rank // 2 * LANES, LANES), LANES)
    top = lax.broadcasted_iota(jnp.int32, (8, LANES), 0) < 4
    tables = [chunk_ref[source, plane, 48:CHUNK].astype(jnp.float32) for source in range(sources)]
    tables.append(folded_ref[48:CHUNK].astype(jnp.float32))
    tables.append(jnp.zeros_like(tables[0]))
    tables = jnp.concatenate(tables, axis=0).astype(jnp.bfloat16)
    for pair in range(2):
        fresh_keys, fresh_values = [], []
        for token in range(3):
            a = token_ref[token, 2 * pair, :, columns].astype(jnp.float32)
            b = token_ref[token, 2 * pair + 1, :, columns].astype(jnp.float32)
            fresh_keys.append(jnp.where(top, a[0:1], b[0:1]))
            fresh_values.append(jnp.where(top, a[1:2], b[1:2]))
        for step in range(3):
            own = []
            for r in (2 * pair, 2 * pair + 1):
                wide = query_ref[step, r, pl.ds(pl.multiple_of(rank // 4 * 16, 16), 16), :].astype(jnp.float32)
                own.append(jnp.where(rank // 2 % 2 == 1, wide[8:], wide[:8]))
            a, b = own
            query = jnp.where(
                rank % 2 == 1,
                jnp.where(top, pltpu.roll(a, 4, 0), b),
                jnp.where(top, a, pltpu.roll(b, 4, 0)),
            )
            index = step * 2 + pair
            stats = jnp.dot(tables, spread_of(index), preferred_element_type=jnp.float32)
            peaks = [stats[8 * source : 8 * source + 8, :LANES] for source in range(sources + 1)]
            totals = [stats[8 * source : 8 * source + 8, LANES:] for source in range(sources + 1)]
            parts = [chunk_ref[source, plane, 8 * index : 8 * index + 8] for source in range(sources)]
            parts.append(folded_ref[8 * index : 8 * index + 8])
            scores = [
                jnp.sum(query * fresh_keys[token], axis=1, keepdims=True) * FACTOR for token in range(step + 1)
            ]
            joint = functools.reduce(jnp.maximum, peaks + scores)
            total = jnp.zeros((8, LANES), jnp.float32)
            summed = jnp.zeros((8, LANES), jnp.float32)
            for peak, share, part in zip(peaks, totals, parts, strict=True):
                scale = jnp.exp(peak - joint)
                total += share * scale
                summed += part.astype(jnp.float32) * scale
            for token in range(step + 1):
                weight = jnp.exp(scores[token] - joint)
                total += weight
                summed += weight.astype(jnp.bfloat16).astype(jnp.float32) * fresh_values[token]
            attended = summed / total
            attended_ref[step, 2 * pair] = attended[:4].astype(jnp.bfloat16)
            attended_ref[step, 2 * pair + 1] = attended[4:].astype(jnp.bfloat16)


def merge(chunks, folded, queries, new_kv):
    steps, req_dev, _, head_dim = queries.shape
    return pl.pallas_call(
        merge_kernel,
        in_specs=[pl.BlockSpec(memory_space=pltpu.VMEM)] * 4,
        out_specs=pl.BlockSpec(memory_space=pltpu.VMEM),
        out_shape=jax.ShapeDtypeStruct((steps, req_dev, 4, head_dim), jnp.bfloat16),
        compiler_params=pltpu.CompilerParams(vmem_limit_bytes=LIMIT),
        name="merge",
    )(chunks, folded, queries, new_kv)


def body(kv_cache, lengths, queries, new_kv, moving_slot, destination, block_index):
    halves = [list(range(HALF)), list(range(HALF, 2 * HALF))]
    planes = [list(range(8)), list(range(8, 16))]
    packed = pack(moving_slot, block_index, kv_cache, new_kv)
    pieces = lax.all_to_all(packed, "replica", 0, 0, tiled=True, axis_index_groups=halves)
    local = front(lengths, kv_cache, queries, packed)
    local, pieces = lax.optimization_barrier((local, pieces))
    chunks = lax.all_to_all(local, "tp", 0, 0, tiled=True, axis_index_groups=planes)
    ordered, half_sum = fold(destination, chunks, pieces)
    folded = lax.ppermute(half_sum, "tp", [(i, i ^ 8) for i in range(16)])
    delivered = lax.all_to_all(ordered, "replica", 0, 0, tiled=True)
    attended = merge(chunks, folded, queries, new_kv)
    arrived, handed = unpack(destination, delivered, kv_cache.shape[-1])
    return (attended, arrived, handed)


def solution(mesh):
    placed = (
        P("replica", None, "tp", None),
        P("replica"),
        P(None, "replica", None, None),
        P(None, "replica", None, None),
        P("replica"),
        P(),
        P("replica"),
    )
    return jax.shard_map(
        body,
        mesh=mesh,
        in_specs=placed,
        out_specs=(
            P(None, "replica", "tp", None),
            P("replica", None, "tp", None),
            P("replica", None, None, None),
        ),
        check_vma=False,
    )
```

```python
import functools
import math

import jax
import jax.numpy as jnp
from jax import lax
from jax.experimental import pallas as pl
from jax.experimental.pallas import tpu as pltpu
from jax.sharding import PartitionSpec as P

BLOCK = 32
HALF = 16
SLOT = 40
CHUNK = 56
LANES = 128
HIDDEN = -1e30
MEMBERS = (13, 11, 15, 10, 5, 29, 24, 4, 22, 19, 27, 20, 3, 2, 14, 25, 9, 18, 12, 31, 16, 28, 7, 26, 21, 1, 23, 17, 30, 8, 0, 6)
NEAR = (8, 2, 0, 15, 1, 13, 12, 9, 3, 7, 4, 10, 14, 11, 6, 5)
PLANE = (6, 7, 2, 4, 0, 3, 1, 5)
FACTOR = 1.0 / math.sqrt(LANES)
LIMIT = 16 << 20
FRONT_LIMIT = 61 << 20


def pack_kernel(slot_ref, block_ref, cache_hbm, token_hbm, sent_ref, moving_ref, token_ref, moving_sem, token_sem):
    slot = slot_ref[0]
    first = pl.multiple_of(block_ref[0] * BLOCK, BLOCK)
    moving_copy = pltpu.make_async_copy(cache_hbm.at[slot, :, pl.ds(first, BLOCK)], moving_ref, moving_sem)
    moving_copy.start()
    token_copy = pltpu.make_async_copy(token_hbm, token_ref, token_sem)
    token_copy.start()
    row = lax.broadcasted_iota(jnp.int32, (8, LANES), 0)
    token_copy.wait()
    lines = [token_ref[step, slot].astype(jnp.float32) for step in range(3)]
    moving_copy.wait()
    for kind in range(2):
        for tile in range(8):
            columns = slice(tile * LANES, (tile + 1) * LANES)
            tokens = jnp.zeros((8, LANES), jnp.float32)
            for step in range(3):
                tokens = jnp.where(row == step, lines[step][kind : kind + 1, columns], tokens)
            sent_ref[NEAR.index(kind * 8 + tile), :BLOCK] = moving_ref[kind, :, columns]
            sent_ref[NEAR.index(kind * 8 + tile), BLOCK:] = tokens.astype(jnp.bfloat16)


def pack(moving_slot, block_index, kv_cache, new_kv):
    return pl.pallas_call(
        pack_kernel,
        in_specs=[
            pl.BlockSpec(memory_space=pltpu.SMEM),
            pl.BlockSpec(memory_space=pltpu.SMEM),
            pl.BlockSpec(memory_space=pl.ANY),
            pl.BlockSpec(memory_space=pl.ANY),
        ],
        out_specs=pl.BlockSpec(memory_space=pltpu.VMEM),
        out_shape=jax.ShapeDtypeStruct((HALF, SLOT, LANES), jnp.bfloat16),
        scratch_shapes=[
            pltpu.VMEM((2, BLOCK, kv_cache.shape[-1]), jnp.bfloat16),
            pltpu.VMEM(new_kv.shape, jnp.bfloat16),
            pltpu.SemaphoreType.DMA(()),
            pltpu.SemaphoreType.DMA(()),
        ],
        compiler_params=pltpu.CompilerParams(vmem_limit_bytes=FRONT_LIMIT),
        name="pack",
    )(moving_slot, block_index, kv_cache, new_kv)


def front_kernel(
    lengths_hbm, cache_hbm, query_hbm, after_ref, local_ref,
    lengths_ref, cache_ref, query_ref, lengths_sem, cache_sem, query_sem,
):
    del after_ref
    requests, _, pos_dev, _ = cache_ref.shape
    lengths_copy = pltpu.make_async_copy(lengths_hbm, lengths_ref, lengths_sem)
    lengths_copy.start()
    query_copy = pltpu.make_async_copy(query_hbm, query_ref, query_sem)
    query_copy.start()
    cache_copies = [
        pltpu.make_async_copy(cache_hbm.at[r], cache_ref.at[r], cache_sem.at[r]) for r in range(requests)
    ]
    for copy in cache_copies:
        copy.start()

    position = lax.axis_index("tp") * pos_dev + lax.broadcasted_iota(jnp.int32, (8, pos_dev), 1)
    lane = lax.broadcasted_iota(jnp.int32, (8, LANES), 1)
    top = lax.broadcasted_iota(jnp.int32, (8, LANES), 0) < 4
    lengths_copy.wait()
    query_copy.wait()

    def attend(r):
        live = position < lengths_ref[r]
        steps = [query_ref[step, r].astype(jnp.float32) for step in range(3)]
        scores = []
        for head in range(8):
            query = jnp.concatenate([part[head * 8 : head * 8 + 8] for part in steps], axis=0)
            scores.append(
                lax.dot_general(
                    query.astype(jnp.bfloat16),
                    cache_ref[r, 0, :, head * LANES : (head + 1) * LANES],
                    (((1,), (1,)), ((), ())),
                    preferred_element_type=jnp.float32,
                )
            )
        results = []
        for head in range(8):
            tiles, stats = [], []
            for step in range(3):
                score = jnp.where(live, scores[head][8 * step : 8 * step + 8] * FACTOR, HIDDEN)
                peak = jnp.max(score, axis=1, keepdims=True)
                weight = jnp.where(live, jnp.exp(score - peak), 0.0)
                total = jnp.sum(weight, axis=1, keepdims=True)
                tiles.append(weight)
                peak_high = peak.astype(jnp.bfloat16).astype(jnp.float32)
                rest = peak - peak_high
                peak_mid = rest.astype(jnp.bfloat16).astype(jnp.float32)
                total_high = total.astype(jnp.bfloat16).astype(jnp.float32)
                stats.append((peak_high, peak_mid, rest - peak_mid, total_high, total - total_high))
            summed = jnp.dot(
                jnp.concatenate(tiles, axis=0).astype(jnp.bfloat16),
                cache_ref[r, 1, :, head * LANES : (head + 1) * LANES],
                preferred_element_type=jnp.float32,
            )
            results.append((summed, stats))
        return results

    for pair in range(2):
        both = []
        for r in (2 * pair, 2 * pair + 1):
            cache_copies[r].wait()
            both.append(attend(r))
        for head in range(8):
            (sum_a, stats_a), (sum_b, stats_b) = both[0][head], both[1][head]
            table_a = jnp.zeros((8, LANES), jnp.float32)
            table_b = jnp.zeros((8, LANES), jnp.float32)
            for step in range(3):
                a, b = sum_a[8 * step : 8 * step + 8], sum_b[8 * step : 8 * step + 8]
                rows = slice(16 * step + 8 * pair, 16 * step + 8 * pair + 8)
                here = (PLANE.index(2 * head % 8), head // 4, rows)
                local_ref[here] = jnp.where(top, a, pltpu.roll(b, 4, 0)).astype(jnp.bfloat16)
                here = (PLANE.index(2 * head % 8 + 1), head // 4, rows)
                local_ref[here] = jnp.where(top, pltpu.roll(a, 4, 0), b).astype(jnp.bfloat16)
                for term in range(5):
                    here = lane == (step * 2 + pair) * 8 + term
                    table_a = jnp.where(here, stats_a[step][term], table_a)
                    table_b = jnp.where(here, stats_b[step][term], table_b)
            for half, table in (
                (0, jnp.where(top, table_a, pltpu.roll(table_b, 4, 0))),
                (1, jnp.where(top, pltpu.roll(table_a, 4, 0), table_b)),
            ):
                here = (PLANE.index(2 * head % 8 + half), head // 4, slice(48, CHUNK))
                if pair == 1:
                    table = table + local_ref[here].astype(jnp.float32)
                local_ref[here] = table.astype(jnp.bfloat16)


def front(lengths, kv_cache, queries, after):
    req_dev = kv_cache.shape[0]
    return pl.pallas_call(
        front_kernel,
        in_specs=[pl.BlockSpec(memory_space=pl.ANY)] * 4,
        out_specs=pl.BlockSpec(memory_space=pltpu.VMEM),
        out_shape=jax.ShapeDtypeStruct((8, 2, CHUNK, LANES), jnp.bfloat16),
        scratch_shapes=[
            pltpu.SMEM(lengths.shape, jnp.int32),
            pltpu.VMEM(kv_cache.shape, jnp.bfloat16),
            pltpu.VMEM(queries.shape, jnp.bfloat16),
            pltpu.SemaphoreType.DMA(()),
            pltpu.SemaphoreType.DMA((req_dev,)),
            pltpu.SemaphoreType.DMA(()),
        ],
        compiler_params=pltpu.CompilerParams(vmem_limit_bytes=FRONT_LIMIT),
        name="front",
    )(lengths, kv_cache, queries, after)


def spread_of(index):
    term = lax.broadcasted_iota(jnp.int32, (LANES, 2 * LANES), 0) - index * 8
    second = lax.broadcasted_iota(jnp.int32, (LANES, 2 * LANES), 1) >= LANES
    maxima = jnp.where((term >= 0) & (term < 3), 1.0, 0.0)
    totals = jnp.where((term == 3) | (term == 4), 1.0, 0.0)
    return jnp.where(second, totals, maxima).astype(jnp.bfloat16)


def order_kernel(destination_ref, piece_ref, slot_ref, source_ref):
    for source in range(2 * HALF):
        source_ref[destination_ref[source]] = NEAR.index(source % HALF)
    for slot, target in enumerate(MEMBERS):
        slot_ref[slot] = piece_ref[source_ref[target]]


def order(destination, pieces):
    return pl.pallas_call(
        order_kernel,
        in_specs=[pl.BlockSpec(memory_space=pltpu.SMEM), pl.BlockSpec(memory_space=pltpu.VMEM)],
        out_specs=pl.BlockSpec(memory_space=pltpu.VMEM),
        out_shape=jax.ShapeDtypeStruct((2 * HALF, SLOT, LANES), jnp.bfloat16),
        scratch_shapes=[pltpu.SMEM((2 * HALF,), jnp.int32)],
        compiler_params=pltpu.CompilerParams(vmem_limit_bytes=LIMIT),
        name="order",
    )(destination, pieces)


def fold_kernel(chunk_ref, out_ref):
    other = 1 - lax.axis_index("tp") // 8
    sources = chunk_ref.shape[0]
    lane = lax.broadcasted_iota(jnp.int32, (8, LANES), 1)
    tables = jnp.concatenate(
        [chunk_ref[source, other, 48:CHUNK].astype(jnp.float32) for source in range(sources)], axis=0
    ).astype(jnp.bfloat16)
    joined = jnp.zeros((8, LANES), jnp.float32)
    for index in range(6):
        stats = jnp.dot(tables, spread_of(index), preferred_element_type=jnp.float32)
        peaks = [stats[8 * source : 8 * source + 8, :LANES] for source in range(sources)]
        totals = [stats[8 * source : 8 * source + 8, LANES:] for source in range(sources)]
        joint = functools.reduce(jnp.maximum, peaks)
        total = jnp.zeros((8, LANES), jnp.float32)
        summed = jnp.zeros((8, LANES), jnp.float32)
        for source in range(sources):
            scale = jnp.exp(peaks[source] - joint)
            total += totals[source] * scale
            part = chunk_ref[source, other, 8 * index : 8 * index + 8]
            summed += part.astype(jnp.float32) * scale
        out_ref[8 * index : 8 * index + 8] = summed.astype(jnp.bfloat16)
        joint_high = joint.astype(jnp.bfloat16).astype(jnp.float32)
        rest = joint - joint_high
        joint_mid = rest.astype(jnp.bfloat16).astype(jnp.float32)
        total_high = total.astype(jnp.bfloat16).astype(jnp.float32)
        terms = (joint_high, joint_mid, rest - joint_mid, total_high, total - total_high)
        for term, value in enumerate(terms):
            joined = jnp.where(lane == index * 8 + term, value, joined)
    out_ref[48:CHUNK] = joined.astype(jnp.bfloat16)


def fold(chunks):
    return pl.pallas_call(
        fold_kernel,
        in_specs=[pl.BlockSpec(memory_space=pltpu.VMEM)],
        out_specs=pl.BlockSpec(memory_space=pltpu.VMEM),
        out_shape=jax.ShapeDtypeStruct((CHUNK, LANES), jnp.bfloat16),
        compiler_params=pltpu.CompilerParams(vmem_limit_bytes=LIMIT),
        name="fold",
    )(chunks)


def unpack_kernel(destination_ref, piece_ref, arrived_ref, handed_ref):
    mine = lax.axis_index("replica")
    upper = jnp.bool_(False)
    for source in range(HALF, 2 * HALF):
        upper = upper | (destination_ref[source] == mine)
    places = [MEMBERS.index(member) for member in range(2 * HALF)]
    places = [jnp.where(upper, places[HALF + piece], places[piece]) for piece in range(HALF)]
    row = lax.broadcasted_iota(jnp.int32, (2, LANES), 0)
    for tile in range(8):
        columns = slice(tile * LANES, (tile + 1) * LANES)
        lines = []
        for kind in range(2):
            arrived_ref[0, kind, :, columns] = piece_ref[places[kind * 8 + tile], :BLOCK]
            lines.append(piece_ref[places[kind * 8 + tile], BLOCK:].astype(jnp.float32))
        for step in range(3):
            both = jnp.where(row == 0, lines[0][step : step + 1], lines[1][step : step + 1])
            handed_ref[0, step, :, columns] = both.astype(jnp.bfloat16)


def unpack(destination, pieces, width):
    return pl.pallas_call(
        unpack_kernel,
        in_specs=[pl.BlockSpec(memory_space=pltpu.SMEM), pl.BlockSpec(memory_space=pltpu.VMEM)],
        out_specs=[pl.BlockSpec(memory_space=pltpu.VMEM)] * 2,
        out_shape=(
            jax.ShapeDtypeStruct((1, 2, BLOCK, width), jnp.bfloat16),
            jax.ShapeDtypeStruct((1, 3, 2, width), jnp.bfloat16),
        ),
        compiler_params=pltpu.CompilerParams(vmem_limit_bytes=LIMIT),
        name="unpack",
    )(destination, pieces)


def merge_kernel(chunk_ref, folded_ref, query_ref, token_ref, attended_ref):
    rank = lax.axis_index("tp")
    sources = chunk_ref.shape[0]
    plane = rank // 8
    columns = pl.ds(pl.multiple_of(rank // 2 * LANES, LANES), LANES)
    top = lax.broadcasted_iota(jnp.int32, (8, LANES), 0) < 4
    tables = [chunk_ref[source, plane, 48:CHUNK].astype(jnp.float32) for source in range(sources)]
    tables.append(folded_ref[48:CHUNK].astype(jnp.float32))
    tables.append(jnp.zeros_like(tables[0]))
    tables = jnp.concatenate(tables, axis=0).astype(jnp.bfloat16)
    for pair in range(2):
        fresh_keys, fresh_values = [], []
        for token in range(3):
            a = token_ref[token, 2 * pair, :, columns].astype(jnp.float32)
            b = token_ref[token, 2 * pair + 1, :, columns].astype(jnp.float32)
            fresh_keys.append(jnp.where(top, a[0:1], b[0:1]))
            fresh_values.append(jnp.where(top, a[1:2], b[1:2]))
        for step in range(3):
            own = []
            for r in (2 * pair, 2 * pair + 1):
                wide = query_ref[step, r, pl.ds(pl.multiple_of(rank // 4 * 16, 16), 16), :].astype(jnp.float32)
                own.append(jnp.where(rank // 2 % 2 == 1, wide[8:], wide[:8]))
            a, b = own
            query = jnp.where(
                rank % 2 == 1,
                jnp.where(top, pltpu.roll(a, 4, 0), b),
                jnp.where(top, a, pltpu.roll(b, 4, 0)),
            )
            index = step * 2 + pair
            stats = jnp.dot(tables, spread_of(index), preferred_element_type=jnp.float32)
            peaks = [stats[8 * source : 8 * source + 8, :LANES] for source in range(sources + 1)]
            totals = [stats[8 * source : 8 * source + 8, LANES:] for source in range(sources + 1)]
            parts = [chunk_ref[source, plane, 8 * index : 8 * index + 8] for source in range(sources)]
            parts.append(folded_ref[8 * index : 8 * index + 8])
            scores = [
                jnp.sum(query * fresh_keys[token], axis=1, keepdims=True) * FACTOR for token in range(step + 1)
            ]
            joint = functools.reduce(jnp.maximum, peaks + scores)
            total = jnp.zeros((8, LANES), jnp.float32)
            summed = jnp.zeros((8, LANES), jnp.float32)
            for peak, share, part in zip(peaks, totals, parts, strict=True):
                scale = jnp.exp(peak - joint)
                total += share * scale
                summed += part.astype(jnp.float32) * scale
            for token in range(step + 1):
                weight = jnp.exp(scores[token] - joint)
                total += weight
                summed += weight.astype(jnp.bfloat16).astype(jnp.float32) * fresh_values[token]
            attended = summed / total
            attended_ref[step, 2 * pair] = attended[:4].astype(jnp.bfloat16)
            attended_ref[step, 2 * pair + 1] = attended[4:].astype(jnp.bfloat16)


def merge(chunks, folded, queries, new_kv):
    steps, req_dev, _, head_dim = queries.shape
    return pl.pallas_call(
        merge_kernel,
        in_specs=[pl.BlockSpec(memory_space=pltpu.VMEM)] * 4,
        out_specs=pl.BlockSpec(memory_space=pltpu.VMEM),
        out_shape=jax.ShapeDtypeStruct((steps, req_dev, 4, head_dim), jnp.bfloat16),
        compiler_params=pltpu.CompilerParams(vmem_limit_bytes=LIMIT),
        name="merge",
    )(chunks, folded, queries, new_kv)


def body(kv_cache, lengths, queries, new_kv, moving_slot, destination, block_index):
    halves = [NEAR, [HALF + member for member in NEAR]]
    planes = [PLANE, [8 + member for member in PLANE]]
    packed = pack(moving_slot, block_index, kv_cache, new_kv)
    pieces = lax.all_to_all(packed, "replica", 0, 0, tiled=True, axis_index_groups=halves)
    local = front(lengths, kv_cache, queries, packed)
    local, pieces = lax.optimization_barrier((local, pieces))
    chunks = lax.all_to_all(local, "tp", 0, 0, tiled=True, axis_index_groups=planes)
    ordered = order(destination, pieces)
    chunks, ordered = lax.optimization_barrier((chunks, ordered))
    delivered = lax.all_to_all(ordered, "replica", 0, 0, tiled=True, axis_index_groups=[MEMBERS])
    folded = lax.ppermute(fold(chunks), "tp", [(i, i ^ 8) for i in range(16)])
    attended = merge(chunks, folded, queries, new_kv)
    arrived, handed = unpack(destination, delivered, kv_cache.shape[-1])
    return (attended, arrived, handed)


def solution(mesh):
    placed = (
        P("replica", None, "tp", None),
        P("replica"),
        P(None, "replica", None, None),
        P(None, "replica", None, None),
        P("replica"),
        P(),
        P("replica"),
    )
    return jax.shard_map(
        body,
        mesh=mesh,
        in_specs=placed,
        out_specs=(
            P(None, "replica", "tp", None),
            P("replica", None, "tp", None),
            P("replica", None, None, None),
        ),
        check_vma=False,
    )
```

```python
import functools
import math

import jax
import jax.numpy as jnp
from jax import lax
from jax.experimental import pallas as pl
from jax.experimental.pallas import tpu as pltpu
from jax.sharding import PartitionSpec as P

BLOCK = 32
HALF = 16
ROWS = 4
CHUNK = 56
LANES = 128
HIDDEN = -1e30
MEMBERS = (16, 14, 13, 26, 28, 18, 29, 25, 11, 6, 10, 2, 31, 19, 8, 17, 15, 3, 4, 1, 7, 9, 20, 30, 22, 5, 12, 27, 23, 21, 0, 24)
NEAR = (8, 2, 0, 15, 1, 13, 12, 9, 3, 7, 4, 10, 14, 11, 6, 5)
PLANE = (6, 7, 2, 4, 0, 3, 1, 5)
FACTOR = 1.0 / math.sqrt(LANES)
LIMIT = 16 << 20
FRONT_LIMIT = 61 << 20


def pack_kernel(slot_ref, block_ref, cache_hbm, token_hbm, sent_ref, moving_ref, token_ref, moving_sem, token_sem):
    slot = slot_ref[0]
    first = pl.multiple_of(block_ref[0] * BLOCK, BLOCK)
    moving_copy = pltpu.make_async_copy(cache_hbm.at[slot, :, pl.ds(first, BLOCK)], moving_ref, moving_sem)
    moving_copy.start()
    token_copy = pltpu.make_async_copy(token_hbm, token_ref, token_sem)
    token_copy.start()
    width = moving_ref.shape[-1]
    row = lax.broadcasted_iota(jnp.int32, (ROWS, LANES), 0)
    token_copy.wait()
    lines = [token_ref[step, slot].astype(jnp.float32) for step in range(3)]
    for piece in range(HALF):
        kind, tile = piece // 8, piece % 8
        tokens = jnp.zeros((ROWS, LANES), jnp.float32)
        for step in range(3):
            line = lines[step][kind : kind + 1, tile * LANES : (tile + 1) * LANES]
            tokens = jnp.where(row == step, line, tokens)
        sent_ref[NEAR.index(piece), :, width:] = tokens.astype(jnp.bfloat16)
    moving_copy.wait()
    for quarter in range(4):
        kind, first = quarter // 2, quarter % 2 * 16
        rows = moving_ref[kind, first : first + 16].astype(jnp.float32)
        for part in range(4):
            piece = NEAR.index(quarter * 4 + part)
            sent_ref[piece, :, :width] = rows[ROWS * part : ROWS * part + ROWS].astype(jnp.bfloat16)


def pack(moving_slot, block_index, kv_cache, new_kv):
    return pl.pallas_call(
        pack_kernel,
        in_specs=[
            pl.BlockSpec(memory_space=pltpu.SMEM),
            pl.BlockSpec(memory_space=pltpu.SMEM),
            pl.BlockSpec(memory_space=pl.ANY),
            pl.BlockSpec(memory_space=pl.ANY),
        ],
        out_specs=pl.BlockSpec(memory_space=pltpu.VMEM),
        out_shape=jax.ShapeDtypeStruct((HALF, ROWS, kv_cache.shape[-1] + LANES), jnp.bfloat16),
        scratch_shapes=[
            pltpu.VMEM((2, BLOCK, kv_cache.shape[-1]), jnp.bfloat16),
            pltpu.VMEM(new_kv.shape, jnp.bfloat16),
            pltpu.SemaphoreType.DMA(()),
            pltpu.SemaphoreType.DMA(()),
        ],
        compiler_params=pltpu.CompilerParams(vmem_limit_bytes=FRONT_LIMIT),
        name="pack",
    )(moving_slot, block_index, kv_cache, new_kv)


def front_kernel(
    lengths_hbm, cache_hbm, query_hbm, after_ref, local_ref,
    lengths_ref, cache_ref, query_ref, lengths_sem, cache_sem, query_sem,
):
    del after_ref
    requests, _, pos_dev, _ = cache_ref.shape
    lengths_copy = pltpu.make_async_copy(lengths_hbm, lengths_ref, lengths_sem)
    lengths_copy.start()
    query_copy = pltpu.make_async_copy(query_hbm, query_ref, query_sem)
    query_copy.start()
    cache_copies = [
        pltpu.make_async_copy(cache_hbm.at[r], cache_ref.at[r], cache_sem.at[r]) for r in range(requests)
    ]
    for copy in cache_copies:
        copy.start()

    position = lax.axis_index("tp") * pos_dev + lax.broadcasted_iota(jnp.int32, (8, pos_dev), 1)
    lane = lax.broadcasted_iota(jnp.int32, (8, LANES), 1)
    top = lax.broadcasted_iota(jnp.int32, (8, LANES), 0) < 4
    lengths_copy.wait()
    query_copy.wait()

    def attend(r):
        live = position < lengths_ref[r]
        steps = [query_ref[step, r].astype(jnp.float32) for step in range(3)]
        scores = []
        for head in range(8):
            query = jnp.concatenate([part[head * 8 : head * 8 + 8] for part in steps], axis=0)
            scores.append(
                lax.dot_general(
                    query.astype(jnp.bfloat16),
                    cache_ref[r, 0, :, head * LANES : (head + 1) * LANES],
                    (((1,), (1,)), ((), ())),
                    preferred_element_type=jnp.float32,
                )
            )
        results = []
        for head in range(8):
            tiles, stats = [], []
            for step in range(3):
                score = jnp.where(live, scores[head][8 * step : 8 * step + 8] * FACTOR, HIDDEN)
                peak = jnp.max(score, axis=1, keepdims=True)
                weight = jnp.where(live, jnp.exp(score - peak), 0.0)
                total = jnp.sum(weight, axis=1, keepdims=True)
                tiles.append(weight)
                peak_high = peak.astype(jnp.bfloat16).astype(jnp.float32)
                rest = peak - peak_high
                peak_mid = rest.astype(jnp.bfloat16).astype(jnp.float32)
                total_high = total.astype(jnp.bfloat16).astype(jnp.float32)
                stats.append((peak_high, peak_mid, rest - peak_mid, total_high, total - total_high))
            summed = jnp.dot(
                jnp.concatenate(tiles, axis=0).astype(jnp.bfloat16),
                cache_ref[r, 1, :, head * LANES : (head + 1) * LANES],
                preferred_element_type=jnp.float32,
            )
            results.append((summed, stats))
        return results

    for pair in range(2):
        both = []
        for r in (2 * pair, 2 * pair + 1):
            cache_copies[r].wait()
            both.append(attend(r))
        for head in range(8):
            (sum_a, stats_a), (sum_b, stats_b) = both[0][head], both[1][head]
            table_a = jnp.zeros((8, LANES), jnp.float32)
            table_b = jnp.zeros((8, LANES), jnp.float32)
            for step in range(3):
                a, b = sum_a[8 * step : 8 * step + 8], sum_b[8 * step : 8 * step + 8]
                rows = slice(16 * step + 8 * pair, 16 * step + 8 * pair + 8)
                here = (PLANE.index(2 * head % 8), head // 4, rows)
                local_ref[here] = jnp.where(top, a, pltpu.roll(b, 4, 0)).astype(jnp.bfloat16)
                here = (PLANE.index(2 * head % 8 + 1), head // 4, rows)
                local_ref[here] = jnp.where(top, pltpu.roll(a, 4, 0), b).astype(jnp.bfloat16)
                for term in range(5):
                    here = lane == (step * 2 + pair) * 8 + term
                    table_a = jnp.where(here, stats_a[step][term], table_a)
                    table_b = jnp.where(here, stats_b[step][term], table_b)
            for half, table in (
                (0, jnp.where(top, table_a, pltpu.roll(table_b, 4, 0))),
                (1, jnp.where(top, pltpu.roll(table_a, 4, 0), table_b)),
            ):
                here = (PLANE.index(2 * head % 8 + half), head // 4, slice(48, CHUNK))
                if pair == 1:
                    table = table + local_ref[here].astype(jnp.float32)
                local_ref[here] = table.astype(jnp.bfloat16)


def front(lengths, kv_cache, queries, after):
    req_dev = kv_cache.shape[0]
    return pl.pallas_call(
        front_kernel,
        in_specs=[pl.BlockSpec(memory_space=pl.ANY)] * 4,
        out_specs=pl.BlockSpec(memory_space=pltpu.VMEM),
        out_shape=jax.ShapeDtypeStruct((8, 2, CHUNK, LANES), jnp.bfloat16),
        scratch_shapes=[
            pltpu.SMEM(lengths.shape, jnp.int32),
            pltpu.VMEM(kv_cache.shape, jnp.bfloat16),
            pltpu.VMEM(queries.shape, jnp.bfloat16),
            pltpu.SemaphoreType.DMA(()),
            pltpu.SemaphoreType.DMA((req_dev,)),
            pltpu.SemaphoreType.DMA(()),
        ],
        compiler_params=pltpu.CompilerParams(vmem_limit_bytes=FRONT_LIMIT),
        name="front",
    )(lengths, kv_cache, queries, after)


def spread_of(index):
    term = lax.broadcasted_iota(jnp.int32, (LANES, 2 * LANES), 0) - index * 8
    second = lax.broadcasted_iota(jnp.int32, (LANES, 2 * LANES), 1) >= LANES
    maxima = jnp.where((term >= 0) & (term < 3), 1.0, 0.0)
    totals = jnp.where((term == 3) | (term == 4), 1.0, 0.0)
    return jnp.where(second, totals, maxima).astype(jnp.bfloat16)


def order_kernel(destination_ref, piece_ref, slot_ref, source_ref):
    for source in range(2 * HALF):
        source_ref[destination_ref[source]] = NEAR.index(source % HALF)
    for slot, target in enumerate(MEMBERS):
        slot_ref[slot] = piece_ref[source_ref[target]]


def order(destination, pieces):
    return pl.pallas_call(
        order_kernel,
        in_specs=[pl.BlockSpec(memory_space=pltpu.SMEM), pl.BlockSpec(memory_space=pltpu.VMEM)],
        out_specs=pl.BlockSpec(memory_space=pltpu.VMEM),
        out_shape=jax.ShapeDtypeStruct((2 * HALF, *pieces.shape[1:]), jnp.bfloat16),
        scratch_shapes=[pltpu.SMEM((2 * HALF,), jnp.int32)],
        compiler_params=pltpu.CompilerParams(vmem_limit_bytes=LIMIT),
        name="order",
    )(destination, pieces)


def fold_kernel(chunk_ref, out_ref):
    other = 1 - lax.axis_index("tp") // 8
    sources = chunk_ref.shape[0]
    lane = lax.broadcasted_iota(jnp.int32, (8, LANES), 1)
    tables = jnp.concatenate(
        [chunk_ref[source, other, 48:CHUNK].astype(jnp.float32) for source in range(sources)], axis=0
    ).astype(jnp.bfloat16)
    joined = jnp.zeros((8, LANES), jnp.float32)
    for index in range(6):
        stats = jnp.dot(tables, spread_of(index), preferred_element_type=jnp.float32)
        peaks = [stats[8 * source : 8 * source + 8, :LANES] for source in range(sources)]
        totals = [stats[8 * source : 8 * source + 8, LANES:] for source in range(sources)]
        joint = functools.reduce(jnp.maximum, peaks)
        total = jnp.zeros((8, LANES), jnp.float32)
        summed = jnp.zeros((8, LANES), jnp.float32)
        for source in range(sources):
            scale = jnp.exp(peaks[source] - joint)
            total += totals[source] * scale
            part = chunk_ref[source, other, 8 * index : 8 * index + 8]
            summed += part.astype(jnp.float32) * scale
        out_ref[8 * index : 8 * index + 8] = summed.astype(jnp.bfloat16)
        joint_high = joint.astype(jnp.bfloat16).astype(jnp.float32)
        rest = joint - joint_high
        joint_mid = rest.astype(jnp.bfloat16).astype(jnp.float32)
        total_high = total.astype(jnp.bfloat16).astype(jnp.float32)
        terms = (joint_high, joint_mid, rest - joint_mid, total_high, total - total_high)
        for term, value in enumerate(terms):
            joined = jnp.where(lane == index * 8 + term, value, joined)
    out_ref[48:CHUNK] = joined.astype(jnp.bfloat16)


def fold(chunks):
    return pl.pallas_call(
        fold_kernel,
        in_specs=[pl.BlockSpec(memory_space=pltpu.VMEM)],
        out_specs=pl.BlockSpec(memory_space=pltpu.VMEM),
        out_shape=jax.ShapeDtypeStruct((CHUNK, LANES), jnp.bfloat16),
        compiler_params=pltpu.CompilerParams(vmem_limit_bytes=LIMIT),
        name="fold",
    )(chunks)


def unpack_kernel(destination_ref, piece_ref, arrived_ref, handed_ref):
    mine = lax.axis_index("replica")
    upper = jnp.bool_(False)
    for source in range(HALF, 2 * HALF):
        upper = upper | (destination_ref[source] == mine)
    places = [MEMBERS.index(member) for member in range(2 * HALF)]
    places = [jnp.where(upper, places[HALF + piece], places[piece]) for piece in range(HALF)]
    width = arrived_ref.shape[-1]
    for quarter in range(4):
        kind, first = quarter // 2, quarter % 2 * 16
        parts = [piece_ref[places[quarter * 4 + part], :, :width].astype(jnp.float32) for part in range(4)]
        arrived_ref[0, kind, first : first + 16] = jnp.concatenate(parts, axis=0).astype(jnp.bfloat16)
    row = lax.broadcasted_iota(jnp.int32, (2, LANES), 0)
    for tile in range(8):
        lines = [piece_ref[places[kind * 8 + tile], :, width:].astype(jnp.float32) for kind in range(2)]
        for step in range(3):
            both = jnp.where(row == 0, lines[0][step : step + 1], lines[1][step : step + 1])
            handed_ref[0, step, :, tile * LANES : (tile + 1) * LANES] = both.astype(jnp.bfloat16)


def unpack(destination, pieces, width):
    return pl.pallas_call(
        unpack_kernel,
        in_specs=[pl.BlockSpec(memory_space=pltpu.SMEM), pl.BlockSpec(memory_space=pltpu.VMEM)],
        out_specs=[pl.BlockSpec(memory_space=pltpu.VMEM)] * 2,
        out_shape=(
            jax.ShapeDtypeStruct((1, 2, BLOCK, width), jnp.bfloat16),
            jax.ShapeDtypeStruct((1, 3, 2, width), jnp.bfloat16),
        ),
        compiler_params=pltpu.CompilerParams(vmem_limit_bytes=LIMIT),
        name="unpack",
    )(destination, pieces)


def own_kernel(chunk_ref, query_ref, token_ref, after_ref, peak_ref, total_ref, summed_ref):
    del after_ref
    rank = lax.axis_index("tp")
    sources = chunk_ref.shape[0]
    plane = rank // 8
    columns = pl.ds(pl.multiple_of(rank // 2 * LANES, LANES), LANES)
    top = lax.broadcasted_iota(jnp.int32, (8, LANES), 0) < 4
    tables = jnp.concatenate(
        [chunk_ref[source, plane, 48:CHUNK].astype(jnp.float32) for source in range(sources)], axis=0
    ).astype(jnp.bfloat16)
    for pair in range(2):
        fresh_keys, fresh_values = [], []
        for token in range(3):
            a = token_ref[token, 2 * pair, :, columns].astype(jnp.float32)
            b = token_ref[token, 2 * pair + 1, :, columns].astype(jnp.float32)
            fresh_keys.append(jnp.where(top, a[0:1], b[0:1]))
            fresh_values.append(jnp.where(top, a[1:2], b[1:2]))
        for step in range(3):
            own = []
            for r in (2 * pair, 2 * pair + 1):
                wide = query_ref[step, r, pl.ds(pl.multiple_of(rank // 4 * 16, 16), 16), :].astype(jnp.float32)
                own.append(jnp.where(rank // 2 % 2 == 1, wide[8:], wide[:8]))
            a, b = own
            query = jnp.where(
                rank % 2 == 1,
                jnp.where(top, pltpu.roll(a, 4, 0), b),
                jnp.where(top, a, pltpu.roll(b, 4, 0)),
            )
            index = step * 2 + pair
            rows = slice(8 * index, 8 * index + 8)
            stats = jnp.dot(tables, spread_of(index), preferred_element_type=jnp.float32)
            peaks = [stats[8 * source : 8 * source + 8, :LANES] for source in range(sources)]
            totals = [stats[8 * source : 8 * source + 8, LANES:] for source in range(sources)]
            scores = [
                jnp.sum(query * fresh_keys[token], axis=1, keepdims=True) * FACTOR for token in range(step + 1)
            ]
            joint = functools.reduce(jnp.maximum, peaks + scores)
            total = jnp.zeros((8, LANES), jnp.float32)
            summed = jnp.zeros((8, LANES), jnp.float32)
            for source in range(sources):
                scale = jnp.exp(peaks[source] - joint)
                total += totals[source] * scale
                summed += chunk_ref[source, plane, rows].astype(jnp.float32) * scale
            for token in range(step + 1):
                weight = jnp.exp(scores[token] - joint)
                total += weight
                summed += weight.astype(jnp.bfloat16).astype(jnp.float32) * fresh_values[token]
            peak_ref[rows], total_ref[rows], summed_ref[rows] = joint, total, summed


def own(chunks, queries, new_kv, after):
    return pl.pallas_call(
        own_kernel,
        in_specs=[pl.BlockSpec(memory_space=pltpu.VMEM)] * 3 + [pl.BlockSpec(memory_space=pl.ANY)],
        out_specs=[pl.BlockSpec(memory_space=pltpu.VMEM)] * 3,
        out_shape=[jax.ShapeDtypeStruct((48, LANES), jnp.float32)] * 3,
        compiler_params=pltpu.CompilerParams(vmem_limit_bytes=LIMIT),
        name="own",
    )(chunks, queries, new_kv, after)


def merge_kernel(peak_ref, total_ref, summed_ref, folded_ref, attended_ref):
    table = folded_ref[48:CHUNK].astype(jnp.float32)
    table = jnp.concatenate([table, table], axis=0).astype(jnp.bfloat16)
    for pair in range(2):
        for step in range(3):
            index = step * 2 + pair
            rows = slice(8 * index, 8 * index + 8)
            stats = jnp.dot(table, spread_of(index), preferred_element_type=jnp.float32)[:8]
            peak = stats[:, :LANES]
            joint = jnp.maximum(peak, peak_ref[rows])
            near, far = jnp.exp(peak_ref[rows] - joint), jnp.exp(peak - joint)
            total = total_ref[rows] * near + stats[:, LANES:] * far
            summed = summed_ref[rows] * near + folded_ref[rows].astype(jnp.float32) * far
            attended = summed / total
            attended_ref[step, 2 * pair] = attended[:4].astype(jnp.bfloat16)
            attended_ref[step, 2 * pair + 1] = attended[4:].astype(jnp.bfloat16)


def merge(parts, folded, shape):
    return pl.pallas_call(
        merge_kernel,
        in_specs=[pl.BlockSpec(memory_space=pltpu.VMEM)] * 4,
        out_specs=pl.BlockSpec(memory_space=pltpu.VMEM),
        out_shape=jax.ShapeDtypeStruct(shape, jnp.bfloat16),
        compiler_params=pltpu.CompilerParams(vmem_limit_bytes=LIMIT),
        name="merge",
    )(*parts, folded)


def body(kv_cache, lengths, queries, new_kv, moving_slot, destination, block_index):
    halves = [NEAR, [HALF + member for member in NEAR]]
    planes = [PLANE, [8 + member for member in PLANE]]
    packed = pack(moving_slot, block_index, kv_cache, new_kv)
    pieces = lax.all_to_all(packed, "replica", 0, 0, tiled=True, axis_index_groups=halves)
    local = front(lengths, kv_cache, queries, packed)
    local, pieces = lax.optimization_barrier((local, pieces))
    chunks = lax.all_to_all(local, "tp", 0, 0, tiled=True, axis_index_groups=planes)
    ordered = order(destination, pieces)
    chunks, ordered = lax.optimization_barrier((chunks, ordered))
    delivered = lax.all_to_all(ordered, "replica", 0, 0, tiled=True, axis_index_groups=[MEMBERS])
    half_sum = fold(chunks)
    folded = lax.ppermute(half_sum, "tp", [(i, i ^ 8) for i in range(16)])
    parts = own(chunks, queries, new_kv, half_sum)
    arrived, handed = unpack(destination, delivered, kv_cache.shape[-1])
    steps, req_dev, _, head_dim = queries.shape
    folded, arrived, handed = lax.optimization_barrier((folded, arrived, handed))
    attended = merge(parts, folded, (steps, req_dev, 4, head_dim))
    return (attended, arrived, handed)


def solution(mesh):
    placed = (
        P("replica", None, "tp", None),
        P("replica"),
        P(None, "replica", None, None),
        P(None, "replica", None, None),
        P("replica"),
        P(),
        P("replica"),
    )
    return jax.shard_map(
        body,
        mesh=mesh,
        in_specs=placed,
        out_specs=(
            P(None, "replica", "tp", None),
            P("replica", None, "tp", None),
            P("replica", None, None, None),
        ),
        check_vma=False,
    )
```

```python
import functools
import math

import jax
import jax.numpy as jnp
from jax import lax
from jax.experimental import pallas as pl
from jax.experimental.pallas import tpu as pltpu
from jax.sharding import PartitionSpec as P

BLOCK = 32
HALF = 16
ROWS = 4
CHUNK = 56
LANES = 128
HIDDEN = -1e30
MEMBERS = (
    (16, 14, 13, 26, 28, 18, 29, 25, 11, 6, 10, 2, 31, 19, 8, 17, 15, 3, 4, 1, 7, 9, 20, 30, 22, 5, 12, 27, 23, 21, 0, 24),
    (12, 3, 9, 28, 11, 5, 4, 6, 0, 27, 31, 14, 23, 18, 30, 1, 10, 16, 29, 21, 2, 17, 20, 8, 22, 15, 13, 7, 19, 26, 25, 24),
)
NEAR = (8, 2, 0, 15, 1, 13, 12, 9, 3, 7, 4, 10, 14, 11, 6, 5)
PLANE = (6, 7, 2, 4, 0, 3, 1, 5)
FACTOR = 1.0 / math.sqrt(LANES)
LIMIT = 16 << 20
FRONT_LIMIT = 61 << 20


def pack_kernel(slot_ref, block_ref, cache_hbm, token_hbm, sent_ref, moving_ref, token_ref, moving_sem, token_sem):
    slot = slot_ref[0]
    first = pl.multiple_of(block_ref[0] * BLOCK, BLOCK)
    moving_copy = pltpu.make_async_copy(cache_hbm.at[slot, :, pl.ds(first, BLOCK)], moving_ref, moving_sem)
    moving_copy.start()
    token_copy = pltpu.make_async_copy(token_hbm, token_ref, token_sem)
    token_copy.start()
    width = moving_ref.shape[-1]
    row = lax.broadcasted_iota(jnp.int32, (ROWS, LANES), 0)
    token_copy.wait()
    lines = [token_ref[step, slot].astype(jnp.float32) for step in range(3)]
    for piece in range(HALF):
        kind, tile = piece // 8, piece % 8
        tokens = jnp.zeros((ROWS, LANES), jnp.float32)
        for step in range(3):
            line = lines[step][kind : kind + 1, tile * LANES : (tile + 1) * LANES]
            tokens = jnp.where(row == step, line, tokens)
        sent_ref[NEAR.index(piece), :, width:] = tokens.astype(jnp.bfloat16)
    moving_copy.wait()
    for quarter in range(4):
        kind, first = quarter // 2, quarter % 2 * 16
        rows = moving_ref[kind, first : first + 16].astype(jnp.float32)
        for part in range(4):
            piece = NEAR.index(quarter * 4 + part)
            sent_ref[piece, :, :width] = rows[ROWS * part : ROWS * part + ROWS].astype(jnp.bfloat16)


def pack(moving_slot, block_index, kv_cache, new_kv):
    return pl.pallas_call(
        pack_kernel,
        in_specs=[
            pl.BlockSpec(memory_space=pltpu.SMEM),
            pl.BlockSpec(memory_space=pltpu.SMEM),
            pl.BlockSpec(memory_space=pl.ANY),
            pl.BlockSpec(memory_space=pl.ANY),
        ],
        out_specs=pl.BlockSpec(memory_space=pltpu.VMEM),
        out_shape=jax.ShapeDtypeStruct((HALF, ROWS, kv_cache.shape[-1] + LANES), jnp.bfloat16),
        scratch_shapes=[
            pltpu.VMEM((2, BLOCK, kv_cache.shape[-1]), jnp.bfloat16),
            pltpu.VMEM(new_kv.shape, jnp.bfloat16),
            pltpu.SemaphoreType.DMA(()),
            pltpu.SemaphoreType.DMA(()),
        ],
        compiler_params=pltpu.CompilerParams(vmem_limit_bytes=FRONT_LIMIT),
        name="pack",
    )(moving_slot, block_index, kv_cache, new_kv)


def front_kernel(
    lengths_hbm, cache_hbm, query_hbm, after_ref, local_ref,
    lengths_ref, cache_ref, query_ref, lengths_sem, cache_sem, query_sem,
):
    del after_ref
    requests, _, pos_dev, _ = cache_ref.shape
    lengths_copy = pltpu.make_async_copy(lengths_hbm, lengths_ref, lengths_sem)
    lengths_copy.start()
    query_copy = pltpu.make_async_copy(query_hbm, query_ref, query_sem)
    query_copy.start()
    cache_copies = [
        pltpu.make_async_copy(cache_hbm.at[r], cache_ref.at[r], cache_sem.at[r]) for r in range(requests)
    ]
    for copy in cache_copies:
        copy.start()

    position = lax.axis_index("tp") * pos_dev + lax.broadcasted_iota(jnp.int32, (8, pos_dev), 1)
    lane = lax.broadcasted_iota(jnp.int32, (8, LANES), 1)
    top = lax.broadcasted_iota(jnp.int32, (8, LANES), 0) < 4
    lengths_copy.wait()
    query_copy.wait()

    def attend(r):
        live = position < lengths_ref[r]
        steps = [query_ref[step, r].astype(jnp.float32) for step in range(3)]
        scores = []
        for head in range(8):
            query = jnp.concatenate([part[head * 8 : head * 8 + 8] for part in steps], axis=0)
            scores.append(
                lax.dot_general(
                    query.astype(jnp.bfloat16),
                    cache_ref[r, 0, :, head * LANES : (head + 1) * LANES],
                    (((1,), (1,)), ((), ())),
                    preferred_element_type=jnp.float32,
                )
            )
        results = []
        for head in range(8):
            tiles, stats = [], []
            for step in range(3):
                score = jnp.where(live, scores[head][8 * step : 8 * step + 8] * FACTOR, HIDDEN)
                peak = jnp.max(score, axis=1, keepdims=True)
                weight = jnp.where(live, jnp.exp(score - peak), 0.0)
                total = jnp.sum(weight, axis=1, keepdims=True)
                tiles.append(weight)
                peak_high = peak.astype(jnp.bfloat16).astype(jnp.float32)
                rest = peak - peak_high
                peak_mid = rest.astype(jnp.bfloat16).astype(jnp.float32)
                total_high = total.astype(jnp.bfloat16).astype(jnp.float32)
                stats.append((peak_high, peak_mid, rest - peak_mid, total_high, total - total_high))
            summed = jnp.dot(
                jnp.concatenate(tiles, axis=0).astype(jnp.bfloat16),
                cache_ref[r, 1, :, head * LANES : (head + 1) * LANES],
                preferred_element_type=jnp.float32,
            )
            results.append((summed, stats))
        return results

    for pair in range(2):
        both = []
        for r in (2 * pair, 2 * pair + 1):
            cache_copies[r].wait()
            both.append(attend(r))
        for head in range(8):
            (sum_a, stats_a), (sum_b, stats_b) = both[0][head], both[1][head]
            table_a = jnp.zeros((8, LANES), jnp.float32)
            table_b = jnp.zeros((8, LANES), jnp.float32)
            for step in range(3):
                a, b = sum_a[8 * step : 8 * step + 8], sum_b[8 * step : 8 * step + 8]
                rows = slice(16 * step + 8 * pair, 16 * step + 8 * pair + 8)
                here = (PLANE.index(2 * head % 8), head // 4, rows)
                local_ref[here] = jnp.where(top, a, pltpu.roll(b, 4, 0)).astype(jnp.bfloat16)
                here = (PLANE.index(2 * head % 8 + 1), head // 4, rows)
                local_ref[here] = jnp.where(top, pltpu.roll(a, 4, 0), b).astype(jnp.bfloat16)
                for term in range(5):
                    here = lane == (step * 2 + pair) * 8 + term
                    table_a = jnp.where(here, stats_a[step][term], table_a)
                    table_b = jnp.where(here, stats_b[step][term], table_b)
            for half, table in (
                (0, jnp.where(top, table_a, pltpu.roll(table_b, 4, 0))),
                (1, jnp.where(top, pltpu.roll(table_a, 4, 0), table_b)),
            ):
                here = (PLANE.index(2 * head % 8 + half), head // 4, slice(48, CHUNK))
                if pair == 1:
                    table = table + local_ref[here].astype(jnp.float32)
                local_ref[here] = table.astype(jnp.bfloat16)


def front(lengths, kv_cache, queries, after):
    req_dev = kv_cache.shape[0]
    return pl.pallas_call(
        front_kernel,
        in_specs=[pl.BlockSpec(memory_space=pl.ANY)] * 4,
        out_specs=pl.BlockSpec(memory_space=pltpu.VMEM),
        out_shape=jax.ShapeDtypeStruct((8, 2, CHUNK, LANES), jnp.bfloat16),
        scratch_shapes=[
            pltpu.SMEM(lengths.shape, jnp.int32),
            pltpu.VMEM(kv_cache.shape, jnp.bfloat16),
            pltpu.VMEM(queries.shape, jnp.bfloat16),
            pltpu.SemaphoreType.DMA(()),
            pltpu.SemaphoreType.DMA((req_dev,)),
            pltpu.SemaphoreType.DMA(()),
        ],
        compiler_params=pltpu.CompilerParams(vmem_limit_bytes=FRONT_LIMIT),
        name="front",
    )(lengths, kv_cache, queries, after)


def spread_of(index):
    term = lax.broadcasted_iota(jnp.int32, (LANES, 2 * LANES), 0) - index * 8
    second = lax.broadcasted_iota(jnp.int32, (LANES, 2 * LANES), 1) >= LANES
    maxima = jnp.where((term >= 0) & (term < 3), 1.0, 0.0)
    totals = jnp.where((term == 3) | (term == 4), 1.0, 0.0)
    return jnp.where(second, totals, maxima).astype(jnp.bfloat16)


def order_kernel(destination_ref, piece_ref, slot_ref, source_ref):
    for source in range(2 * HALF):
        source_ref[destination_ref[source]] = NEAR.index(source % HALF)
    lower = lax.axis_index("tp") < 8
    for slot, targets in enumerate(zip(*MEMBERS, strict=True)):
        slot_ref[slot] = piece_ref[source_ref[jnp.where(lower, targets[0], targets[1])]]


def order(destination, pieces):
    return pl.pallas_call(
        order_kernel,
        in_specs=[pl.BlockSpec(memory_space=pltpu.SMEM), pl.BlockSpec(memory_space=pltpu.VMEM)],
        out_specs=pl.BlockSpec(memory_space=pltpu.VMEM),
        out_shape=jax.ShapeDtypeStruct((2 * HALF, *pieces.shape[1:]), jnp.bfloat16),
        scratch_shapes=[pltpu.SMEM((2 * HALF,), jnp.int32)],
        compiler_params=pltpu.CompilerParams(vmem_limit_bytes=LIMIT),
        name="order",
    )(destination, pieces)


def fold_kernel(chunk_ref, out_ref):
    other = 1 - lax.axis_index("tp") // 8
    sources = chunk_ref.shape[0]
    lane = lax.broadcasted_iota(jnp.int32, (8, LANES), 1)
    tables = jnp.concatenate(
        [chunk_ref[source, other, 48:CHUNK].astype(jnp.float32) for source in range(sources)], axis=0
    ).astype(jnp.bfloat16)
    joined = jnp.zeros((8, LANES), jnp.float32)
    for index in range(6):
        stats = jnp.dot(tables, spread_of(index), preferred_element_type=jnp.float32)
        peaks = [stats[8 * source : 8 * source + 8, :LANES] for source in range(sources)]
        totals = [stats[8 * source : 8 * source + 8, LANES:] for source in range(sources)]
        joint = functools.reduce(jnp.maximum, peaks)
        total = jnp.zeros((8, LANES), jnp.float32)
        summed = jnp.zeros((8, LANES), jnp.float32)
        for source in range(sources):
            scale = jnp.exp(peaks[source] - joint)
            total += totals[source] * scale
            part = chunk_ref[source, other, 8 * index : 8 * index + 8]
            summed += part.astype(jnp.float32) * scale
        out_ref[8 * index : 8 * index + 8] = summed.astype(jnp.bfloat16)
        joint_high = joint.astype(jnp.bfloat16).astype(jnp.float32)
        rest = joint - joint_high
        joint_mid = rest.astype(jnp.bfloat16).astype(jnp.float32)
        total_high = total.astype(jnp.bfloat16).astype(jnp.float32)
        terms = (joint_high, joint_mid, rest - joint_mid, total_high, total - total_high)
        for term, value in enumerate(terms):
            joined = jnp.where(lane == index * 8 + term, value, joined)
    out_ref[48:CHUNK] = joined.astype(jnp.bfloat16)


def fold(chunks):
    return pl.pallas_call(
        fold_kernel,
        in_specs=[pl.BlockSpec(memory_space=pltpu.VMEM)],
        out_specs=pl.BlockSpec(memory_space=pltpu.VMEM),
        out_shape=jax.ShapeDtypeStruct((CHUNK, LANES), jnp.bfloat16),
        compiler_params=pltpu.CompilerParams(vmem_limit_bytes=LIMIT),
        name="fold",
    )(chunks)


def unpack_kernel(destination_ref, piece_ref, arrived_ref, handed_ref):
    mine = lax.axis_index("replica")
    upper = jnp.bool_(False)
    for source in range(HALF, 2 * HALF):
        upper = upper | (destination_ref[source] == mine)
    lower = lax.axis_index("tp") < 8
    places = [
        jnp.where(lower, MEMBERS[0].index(member), MEMBERS[1].index(member)) for member in range(2 * HALF)
    ]
    places = [jnp.where(upper, places[HALF + piece], places[piece]) for piece in range(HALF)]
    width = arrived_ref.shape[-1]
    for quarter in range(4):
        kind, first = quarter // 2, quarter % 2 * 16
        parts = [piece_ref[places[quarter * 4 + part], :, :width].astype(jnp.float32) for part in range(4)]
        arrived_ref[0, kind, first : first + 16] = jnp.concatenate(parts, axis=0).astype(jnp.bfloat16)
    row = lax.broadcasted_iota(jnp.int32, (2, LANES), 0)
    for tile in range(8):
        lines = [piece_ref[places[kind * 8 + tile], :, width:].astype(jnp.float32) for kind in range(2)]
        for step in range(3):
            both = jnp.where(row == 0, lines[0][step : step + 1], lines[1][step : step + 1])
            handed_ref[0, step, :, tile * LANES : (tile + 1) * LANES] = both.astype(jnp.bfloat16)


def unpack(destination, pieces, width):
    return pl.pallas_call(
        unpack_kernel,
        in_specs=[pl.BlockSpec(memory_space=pltpu.SMEM), pl.BlockSpec(memory_space=pltpu.VMEM)],
        out_specs=[pl.BlockSpec(memory_space=pltpu.VMEM)] * 2,
        out_shape=(
            jax.ShapeDtypeStruct((1, 2, BLOCK, width), jnp.bfloat16),
            jax.ShapeDtypeStruct((1, 3, 2, width), jnp.bfloat16),
        ),
        compiler_params=pltpu.CompilerParams(vmem_limit_bytes=LIMIT),
        name="unpack",
    )(destination, pieces)


def own_kernel(chunk_ref, query_ref, token_ref, after_ref, peak_ref, total_ref, summed_ref):
    del after_ref
    rank = lax.axis_index("tp")
    sources = chunk_ref.shape[0]
    plane = rank // 8
    columns = pl.ds(pl.multiple_of(rank // 2 * LANES, LANES), LANES)
    top = lax.broadcasted_iota(jnp.int32, (8, LANES), 0) < 4
    tables = jnp.concatenate(
        [chunk_ref[source, plane, 48:CHUNK].astype(jnp.float32) for source in range(sources)], axis=0
    ).astype(jnp.bfloat16)
    for pair in range(2):
        fresh_keys, fresh_values = [], []
        for token in range(3):
            a = token_ref[token, 2 * pair, :, columns].astype(jnp.float32)
            b = token_ref[token, 2 * pair + 1, :, columns].astype(jnp.float32)
            fresh_keys.append(jnp.where(top, a[0:1], b[0:1]))
            fresh_values.append(jnp.where(top, a[1:2], b[1:2]))
        for step in range(3):
            own = []
            for r in (2 * pair, 2 * pair + 1):
                wide = query_ref[step, r, pl.ds(pl.multiple_of(rank // 4 * 16, 16), 16), :].astype(jnp.float32)
                own.append(jnp.where(rank // 2 % 2 == 1, wide[8:], wide[:8]))
            a, b = own
            query = jnp.where(
                rank % 2 == 1,
                jnp.where(top, pltpu.roll(a, 4, 0), b),
                jnp.where(top, a, pltpu.roll(b, 4, 0)),
            )
            index = step * 2 + pair
            rows = slice(8 * index, 8 * index + 8)
            stats = jnp.dot(tables, spread_of(index), preferred_element_type=jnp.float32)
            peaks = [stats[8 * source : 8 * source + 8, :LANES] for source in range(sources)]
            totals = [stats[8 * source : 8 * source + 8, LANES:] for source in range(sources)]
            scores = [
                jnp.sum(query * fresh_keys[token], axis=1, keepdims=True) * FACTOR for token in range(step + 1)
            ]
            joint = functools.reduce(jnp.maximum, peaks + scores)
            total = jnp.zeros((8, LANES), jnp.float32)
            summed = jnp.zeros((8, LANES), jnp.float32)
            for source in range(sources):
                scale = jnp.exp(peaks[source] - joint)
                total += totals[source] * scale
                summed += chunk_ref[source, plane, rows].astype(jnp.float32) * scale
            for token in range(step + 1):
                weight = jnp.exp(scores[token] - joint)
                total += weight
                summed += weight.astype(jnp.bfloat16).astype(jnp.float32) * fresh_values[token]
            peak_ref[rows], total_ref[rows], summed_ref[rows] = joint, total, summed


def own(chunks, queries, new_kv, after):
    return pl.pallas_call(
        own_kernel,
        in_specs=[pl.BlockSpec(memory_space=pltpu.VMEM)] * 3 + [pl.BlockSpec(memory_space=pl.ANY)],
        out_specs=[pl.BlockSpec(memory_space=pltpu.VMEM)] * 3,
        out_shape=[jax.ShapeDtypeStruct((48, LANES), jnp.float32)] * 3,
        compiler_params=pltpu.CompilerParams(vmem_limit_bytes=LIMIT),
        name="own",
    )(chunks, queries, new_kv, after)


def merge_kernel(peak_ref, total_ref, summed_ref, folded_ref, attended_ref):
    table = folded_ref[48:CHUNK].astype(jnp.float32)
    table = jnp.concatenate([table, table], axis=0).astype(jnp.bfloat16)
    for pair in range(2):
        for step in range(3):
            index = step * 2 + pair
            rows = slice(8 * index, 8 * index + 8)
            stats = jnp.dot(table, spread_of(index), preferred_element_type=jnp.float32)[:8]
            peak = stats[:, :LANES]
            joint = jnp.maximum(peak, peak_ref[rows])
            near, far = jnp.exp(peak_ref[rows] - joint), jnp.exp(peak - joint)
            total = total_ref[rows] * near + stats[:, LANES:] * far
            summed = summed_ref[rows] * near + folded_ref[rows].astype(jnp.float32) * far
            attended = summed / total
            attended_ref[step, 2 * pair] = attended[:4].astype(jnp.bfloat16)
            attended_ref[step, 2 * pair + 1] = attended[4:].astype(jnp.bfloat16)


def merge(parts, folded, shape):
    return pl.pallas_call(
        merge_kernel,
        in_specs=[pl.BlockSpec(memory_space=pltpu.VMEM)] * 4,
        out_specs=pl.BlockSpec(memory_space=pltpu.VMEM),
        out_shape=jax.ShapeDtypeStruct(shape, jnp.bfloat16),
        compiler_params=pltpu.CompilerParams(vmem_limit_bytes=LIMIT),
        name="merge",
    )(*parts, folded)


def body(kv_cache, lengths, queries, new_kv, moving_slot, destination, block_index):
    halves = [NEAR, [HALF + member for member in NEAR]]
    planes = [PLANE, [8 + member for member in PLANE]]
    packed = pack(moving_slot, block_index, kv_cache, new_kv)
    pieces = lax.all_to_all(packed, "replica", 0, 0, tiled=True, axis_index_groups=halves)
    local = front(lengths, kv_cache, queries, packed)
    local, pieces = lax.optimization_barrier((local, pieces))
    chunks = lax.all_to_all(local, "tp", 0, 0, tiled=True, axis_index_groups=planes)
    ordered = order(destination, pieces)
    chunks, ordered = lax.optimization_barrier((chunks, ordered))
    tp_count = lax.axis_size("tp")
    groups = [[member * tp_count + t for member in MEMBERS[t // 8]] for t in range(tp_count)]
    delivered = lax.all_to_all(ordered, ("replica", "tp"), 0, 0, tiled=True, axis_index_groups=groups)
    half_sum = fold(chunks)
    folded = lax.ppermute(half_sum, "tp", [(i, i ^ 8) for i in range(16)])
    parts = own(chunks, queries, new_kv, half_sum)
    arrived, handed = unpack(destination, delivered, kv_cache.shape[-1])
    steps, req_dev, _, head_dim = queries.shape
    folded, arrived, handed = lax.optimization_barrier((folded, arrived, handed))
    attended = merge(parts, folded, (steps, req_dev, 4, head_dim))
    return (attended, arrived, handed)


def solution(mesh):
    placed = (
        P("replica", None, "tp", None),
        P("replica"),
        P(None, "replica", None, None),
        P(None, "replica", None, None),
        P("replica"),
        P(),
        P("replica"),
    )
    return jax.shard_map(
        body,
        mesh=mesh,
        in_specs=placed,
        out_specs=(
            P(None, "replica", "tp", None),
            P("replica", None, "tp", None),
            P("replica", None, None, None),
        ),
        check_vma=False,
    )
```

```python
import functools
import math

import jax
import jax.numpy as jnp
from jax import lax
from jax.experimental import pallas as pl
from jax.experimental.pallas import tpu as pltpu
from jax.sharding import PartitionSpec as P

BLOCK = 32
HALF = 16
ROWS = 4
CHUNK = 56
LANES = 128
HIDDEN = -1e30
MEMBERS = (
    (16, 25, 18, 31, 29, 20, 0, 4, 10, 7, 14, 17, 22, 28, 15, 12, 13, 27, 1, 24, 6, 19, 8, 9, 21, 23, 5, 26, 11, 30, 2, 3),
    (12, 3, 9, 28, 11, 5, 4, 6, 0, 27, 31, 14, 23, 18, 30, 1, 10, 16, 29, 21, 2, 17, 20, 8, 22, 15, 13, 7, 19, 26, 25, 24),
)
NEAR = (8, 2, 0, 15, 1, 13, 12, 9, 3, 7, 4, 10, 14, 11, 6, 5)
PLANE = (6, 7, 2, 4, 0, 3, 1, 5)
FACTOR = 1.0 / math.sqrt(LANES)
LIMIT = 16 << 20
FRONT_LIMIT = 61 << 20


def pack_kernel(slot_ref, block_ref, cache_hbm, token_hbm, sent_ref, moving_ref, token_ref, moving_sem, token_sem):
    slot = slot_ref[0]
    first = pl.multiple_of(block_ref[0] * BLOCK, BLOCK)
    moving_copy = pltpu.make_async_copy(cache_hbm.at[slot, :, pl.ds(first, BLOCK)], moving_ref, moving_sem)
    moving_copy.start()
    token_copy = pltpu.make_async_copy(token_hbm.at[:, slot], token_ref, token_sem)
    token_copy.start()
    width = moving_ref.shape[-1]
    row = lax.broadcasted_iota(jnp.int32, (ROWS, LANES), 0)
    token_copy.wait()
    lines = [token_ref[step].astype(jnp.float32) for step in range(3)]
    for piece in range(HALF):
        kind, tile = piece // 8, piece % 8
        tokens = jnp.zeros((ROWS, LANES), jnp.float32)
        for step in range(3):
            line = lines[step][kind : kind + 1, tile * LANES : (tile + 1) * LANES]
            tokens = jnp.where(row == step, line, tokens)
        sent_ref[NEAR.index(piece), :, width:] = tokens.astype(jnp.bfloat16)
    moving_copy.wait()
    for quarter in range(4):
        kind, first = quarter // 2, quarter % 2 * 16
        rows = moving_ref[kind, first : first + 16].astype(jnp.float32)
        for part in range(4):
            piece = NEAR.index(quarter * 4 + part)
            sent_ref[piece, :, :width] = rows[ROWS * part : ROWS * part + ROWS].astype(jnp.bfloat16)


def pack(moving_slot, block_index, kv_cache, new_kv):
    return pl.pallas_call(
        pack_kernel,
        in_specs=[
            pl.BlockSpec(memory_space=pltpu.SMEM),
            pl.BlockSpec(memory_space=pltpu.SMEM),
            pl.BlockSpec(memory_space=pl.ANY),
            pl.BlockSpec(memory_space=pl.ANY),
        ],
        out_specs=pl.BlockSpec(memory_space=pltpu.VMEM),
        out_shape=jax.ShapeDtypeStruct((HALF, ROWS, kv_cache.shape[-1] + LANES), jnp.bfloat16),
        scratch_shapes=[
            pltpu.VMEM((2, BLOCK, kv_cache.shape[-1]), jnp.bfloat16),
            pltpu.VMEM((3, 2, new_kv.shape[-1]), jnp.bfloat16),
            pltpu.SemaphoreType.DMA(()),
            pltpu.SemaphoreType.DMA(()),
        ],
        compiler_params=pltpu.CompilerParams(vmem_limit_bytes=FRONT_LIMIT),
        name="pack",
    )(moving_slot, block_index, kv_cache, new_kv)


def front_kernel(
    lengths_hbm, cache_hbm, query_hbm, after_ref, local_ref,
    lengths_ref, cache_ref, query_ref, lengths_sem, cache_sem, query_sem,
):
    del after_ref
    requests, _, pos_dev, _ = cache_ref.shape
    lengths_copy = pltpu.make_async_copy(lengths_hbm, lengths_ref, lengths_sem)
    lengths_copy.start()
    query_copy = pltpu.make_async_copy(query_hbm, query_ref, query_sem)
    query_copy.start()
    cache_copies = [
        pltpu.make_async_copy(cache_hbm.at[r], cache_ref.at[r], cache_sem.at[r]) for r in range(requests)
    ]
    for copy in cache_copies:
        copy.start()

    position = lax.axis_index("tp") * pos_dev + lax.broadcasted_iota(jnp.int32, (8, pos_dev), 1)
    lane = lax.broadcasted_iota(jnp.int32, (8, LANES), 1)
    top = lax.broadcasted_iota(jnp.int32, (8, LANES), 0) < 4
    lengths_copy.wait()
    query_copy.wait()

    def attend(r):
        live = position < lengths_ref[r]
        steps = [query_ref[step, r].astype(jnp.float32) for step in range(3)]
        scores = []
        for head in range(8):
            query = jnp.concatenate([part[head * 8 : head * 8 + 8] for part in steps], axis=0)
            scores.append(
                lax.dot_general(
                    query.astype(jnp.bfloat16),
                    cache_ref[r, 0, :, head * LANES : (head + 1) * LANES],
                    (((1,), (1,)), ((), ())),
                    preferred_element_type=jnp.float32,
                )
            )
        results = []
        for head in range(8):
            tiles, stats = [], []
            for step in range(3):
                score = jnp.where(live, scores[head][8 * step : 8 * step + 8] * FACTOR, HIDDEN)
                peak = jnp.max(score, axis=1, keepdims=True)
                weight = jnp.where(live, jnp.exp(score - peak), 0.0)
                total = jnp.sum(weight, axis=1, keepdims=True)
                tiles.append(weight)
                peak_high = peak.astype(jnp.bfloat16).astype(jnp.float32)
                rest = peak - peak_high
                peak_mid = rest.astype(jnp.bfloat16).astype(jnp.float32)
                total_high = total.astype(jnp.bfloat16).astype(jnp.float32)
                stats.append((peak_high, peak_mid, rest - peak_mid, total_high, total - total_high))
            summed = jnp.dot(
                jnp.concatenate(tiles, axis=0).astype(jnp.bfloat16),
                cache_ref[r, 1, :, head * LANES : (head + 1) * LANES],
                preferred_element_type=jnp.float32,
            )
            results.append((summed, stats))
        return results

    for pair in range(2):
        both = []
        for r in (2 * pair, 2 * pair + 1):
            cache_copies[r].wait()
            both.append(attend(r))
        for head in range(8):
            (sum_a, stats_a), (sum_b, stats_b) = both[0][head], both[1][head]
            table_a = jnp.zeros((8, LANES), jnp.float32)
            table_b = jnp.zeros((8, LANES), jnp.float32)
            for step in range(3):
                a, b = sum_a[8 * step : 8 * step + 8], sum_b[8 * step : 8 * step + 8]
                rows = slice(16 * step + 8 * pair, 16 * step + 8 * pair + 8)
                here = (PLANE.index(2 * head % 8), head // 4, rows)
                local_ref[here] = jnp.where(top, a, pltpu.roll(b, 4, 0)).astype(jnp.bfloat16)
                here = (PLANE.index(2 * head % 8 + 1), head // 4, rows)
                local_ref[here] = jnp.where(top, pltpu.roll(a, 4, 0), b).astype(jnp.bfloat16)
                for term in range(5):
                    here = lane == (step * 2 + pair) * 8 + term
                    table_a = jnp.where(here, stats_a[step][term], table_a)
                    table_b = jnp.where(here, stats_b[step][term], table_b)
            for half, table in (
                (0, jnp.where(top, table_a, pltpu.roll(table_b, 4, 0))),
                (1, jnp.where(top, pltpu.roll(table_a, 4, 0), table_b)),
            ):
                here = (PLANE.index(2 * head % 8 + half), head // 4, slice(48, CHUNK))
                if pair == 1:
                    table = table + local_ref[here].astype(jnp.float32)
                local_ref[here] = table.astype(jnp.bfloat16)


def front(lengths, kv_cache, queries, after):
    req_dev = kv_cache.shape[0]
    return pl.pallas_call(
        front_kernel,
        in_specs=[pl.BlockSpec(memory_space=pl.ANY)] * 4,
        out_specs=pl.BlockSpec(memory_space=pltpu.VMEM),
        out_shape=jax.ShapeDtypeStruct((8, 2, CHUNK, LANES), jnp.bfloat16),
        scratch_shapes=[
            pltpu.SMEM(lengths.shape, jnp.int32),
            pltpu.VMEM(kv_cache.shape, jnp.bfloat16),
            pltpu.VMEM(queries.shape, jnp.bfloat16),
            pltpu.SemaphoreType.DMA(()),
            pltpu.SemaphoreType.DMA((req_dev,)),
            pltpu.SemaphoreType.DMA(()),
        ],
        compiler_params=pltpu.CompilerParams(vmem_limit_bytes=FRONT_LIMIT),
        name="front",
    )(lengths, kv_cache, queries, after)


def spread_of(index):
    term = lax.broadcasted_iota(jnp.int32, (LANES, 2 * LANES), 0) - index * 8
    second = lax.broadcasted_iota(jnp.int32, (LANES, 2 * LANES), 1) >= LANES
    maxima = jnp.where((term >= 0) & (term < 3), 1.0, 0.0)
    totals = jnp.where((term == 3) | (term == 4), 1.0, 0.0)
    return jnp.where(second, totals, maxima).astype(jnp.bfloat16)


def order_kernel(destination_ref, piece_ref, slot_ref, source_ref):
    for source in range(2 * HALF):
        source_ref[destination_ref[source]] = NEAR.index(source % HALF)
    lower = lax.axis_index("tp") < 8
    for slot, targets in enumerate(zip(*MEMBERS, strict=True)):
        slot_ref[slot] = piece_ref[source_ref[jnp.where(lower, targets[0], targets[1])]]


def order(destination, pieces):
    return pl.pallas_call(
        order_kernel,
        in_specs=[pl.BlockSpec(memory_space=pltpu.SMEM), pl.BlockSpec(memory_space=pltpu.VMEM)],
        out_specs=pl.BlockSpec(memory_space=pltpu.VMEM),
        out_shape=jax.ShapeDtypeStruct((2 * HALF, *pieces.shape[1:]), jnp.bfloat16),
        scratch_shapes=[pltpu.SMEM((2 * HALF,), jnp.int32)],
        compiler_params=pltpu.CompilerParams(vmem_limit_bytes=LIMIT),
        name="order",
    )(destination, pieces)


def fold_kernel(chunk_ref, out_ref):
    other = 1 - lax.axis_index("tp") // 8
    sources = chunk_ref.shape[0]
    lane = lax.broadcasted_iota(jnp.int32, (8, LANES), 1)
    tables = jnp.concatenate(
        [chunk_ref[source, other, 48:CHUNK].astype(jnp.float32) for source in range(sources)], axis=0
    ).astype(jnp.bfloat16)
    joined = jnp.zeros((8, LANES), jnp.float32)
    for index in range(6):
        stats = jnp.dot(tables, spread_of(index), preferred_element_type=jnp.float32)
        peaks = [stats[8 * source : 8 * source + 8, :LANES] for source in range(sources)]
        totals = [stats[8 * source : 8 * source + 8, LANES:] for source in range(sources)]
        joint = functools.reduce(jnp.maximum, peaks)
        total = jnp.zeros((8, LANES), jnp.float32)
        summed = jnp.zeros((8, LANES), jnp.float32)
        for source in range(sources):
            scale = jnp.exp(peaks[source] - joint)
            total += totals[source] * scale
            part = chunk_ref[source, other, 8 * index : 8 * index + 8]
            summed += part.astype(jnp.float32) * scale
        out_ref[8 * index : 8 * index + 8] = summed.astype(jnp.bfloat16)
        joint_high = joint.astype(jnp.bfloat16).astype(jnp.float32)
        rest = joint - joint_high
        joint_mid = rest.astype(jnp.bfloat16).astype(jnp.float32)
        total_high = total.astype(jnp.bfloat16).astype(jnp.float32)
        terms = (joint_high, joint_mid, rest - joint_mid, total_high, total - total_high)
        for term, value in enumerate(terms):
            joined = jnp.where(lane == index * 8 + term, value, joined)
    out_ref[48:CHUNK] = joined.astype(jnp.bfloat16)


def fold(chunks):
    return pl.pallas_call(
        fold_kernel,
        in_specs=[pl.BlockSpec(memory_space=pltpu.VMEM)],
        out_specs=pl.BlockSpec(memory_space=pltpu.VMEM),
        out_shape=jax.ShapeDtypeStruct((CHUNK, LANES), jnp.bfloat16),
        compiler_params=pltpu.CompilerParams(vmem_limit_bytes=LIMIT),
        name="fold",
    )(chunks)


def unpack_kernel(destination_ref, piece_ref, arrived_ref, handed_ref):
    mine = lax.axis_index("replica")
    upper = jnp.bool_(False)
    for source in range(HALF, 2 * HALF):
        upper = upper | (destination_ref[source] == mine)
    lower = lax.axis_index("tp") < 8
    places = [
        jnp.where(lower, MEMBERS[0].index(member), MEMBERS[1].index(member)) for member in range(2 * HALF)
    ]
    places = [jnp.where(upper, places[HALF + piece], places[piece]) for piece in range(HALF)]
    width = arrived_ref.shape[-1]
    for quarter in range(4):
        kind, first = quarter // 2, quarter % 2 * 16
        parts = [piece_ref[places[quarter * 4 + part], :, :width].astype(jnp.float32) for part in range(4)]
        arrived_ref[0, kind, first : first + 16] = jnp.concatenate(parts, axis=0).astype(jnp.bfloat16)
    row = lax.broadcasted_iota(jnp.int32, (2, LANES), 0)
    for tile in range(8):
        lines = [piece_ref[places[kind * 8 + tile], :, width:].astype(jnp.float32) for kind in range(2)]
        for step in range(3):
            both = jnp.where(row == 0, lines[0][step : step + 1], lines[1][step : step + 1])
            handed_ref[0, step, :, tile * LANES : (tile + 1) * LANES] = both.astype(jnp.bfloat16)


def unpack(destination, pieces, width):
    return pl.pallas_call(
        unpack_kernel,
        in_specs=[pl.BlockSpec(memory_space=pltpu.SMEM), pl.BlockSpec(memory_space=pltpu.VMEM)],
        out_specs=[pl.BlockSpec(memory_space=pltpu.VMEM)] * 2,
        out_shape=(
            jax.ShapeDtypeStruct((1, 2, BLOCK, width), jnp.bfloat16),
            jax.ShapeDtypeStruct((1, 3, 2, width), jnp.bfloat16),
        ),
        compiler_params=pltpu.CompilerParams(vmem_limit_bytes=LIMIT),
        name="unpack",
    )(destination, pieces)


def own_kernel(chunk_ref, query_ref, token_ref, after_ref, peak_ref, total_ref, summed_ref):
    del after_ref
    rank = lax.axis_index("tp")
    sources = chunk_ref.shape[0]
    plane = rank // 8
    columns = pl.ds(pl.multiple_of(rank // 2 * LANES, LANES), LANES)
    top = lax.broadcasted_iota(jnp.int32, (8, LANES), 0) < 4
    tables = jnp.concatenate(
        [chunk_ref[source, plane, 48:CHUNK].astype(jnp.float32) for source in range(sources)], axis=0
    ).astype(jnp.bfloat16)
    for pair in range(2):
        fresh_keys, fresh_values = [], []
        for token in range(3):
            a = token_ref[token, 2 * pair, :, columns].astype(jnp.float32)
            b = token_ref[token, 2 * pair + 1, :, columns].astype(jnp.float32)
            fresh_keys.append(jnp.where(top, a[0:1], b[0:1]))
            fresh_values.append(jnp.where(top, a[1:2], b[1:2]))
        for step in range(3):
            own = []
            for r in (2 * pair, 2 * pair + 1):
                wide = query_ref[step, r, pl.ds(pl.multiple_of(rank // 4 * 16, 16), 16), :].astype(jnp.float32)
                own.append(jnp.where(rank // 2 % 2 == 1, wide[8:], wide[:8]))
            a, b = own
            query = jnp.where(
                rank % 2 == 1,
                jnp.where(top, pltpu.roll(a, 4, 0), b),
                jnp.where(top, a, pltpu.roll(b, 4, 0)),
            )
            index = step * 2 + pair
            rows = slice(8 * index, 8 * index + 8)
            stats = jnp.dot(tables, spread_of(index), preferred_element_type=jnp.float32)
            peaks = [stats[8 * source : 8 * source + 8, :LANES] for source in range(sources)]
            totals = [stats[8 * source : 8 * source + 8, LANES:] for source in range(sources)]
            scores = [
                jnp.sum(query * fresh_keys[token], axis=1, keepdims=True) * FACTOR for token in range(step + 1)
            ]
            joint = functools.reduce(jnp.maximum, peaks + scores)
            total = jnp.zeros((8, LANES), jnp.float32)
            summed = jnp.zeros((8, LANES), jnp.float32)
            for source in range(sources):
                scale = jnp.exp(peaks[source] - joint)
                total += totals[source] * scale
                summed += chunk_ref[source, plane, rows].astype(jnp.float32) * scale
            for token in range(step + 1):
                weight = jnp.exp(scores[token] - joint)
                total += weight
                summed += weight.astype(jnp.bfloat16).astype(jnp.float32) * fresh_values[token]
            peak_ref[rows], total_ref[rows], summed_ref[rows] = joint, total, summed


def own(chunks, queries, new_kv, after):
    return pl.pallas_call(
        own_kernel,
        in_specs=[pl.BlockSpec(memory_space=pltpu.VMEM)] * 3 + [pl.BlockSpec(memory_space=pl.ANY)],
        out_specs=[pl.BlockSpec(memory_space=pltpu.VMEM)] * 3,
        out_shape=[jax.ShapeDtypeStruct((48, LANES), jnp.float32)] * 3,
        compiler_params=pltpu.CompilerParams(vmem_limit_bytes=LIMIT),
        name="own",
    )(chunks, queries, new_kv, after)


def merge_kernel(peak_ref, total_ref, summed_ref, folded_ref, attended_ref):
    table = folded_ref[48:CHUNK].astype(jnp.float32)
    table = jnp.concatenate([table, table], axis=0).astype(jnp.bfloat16)
    for pair in range(2):
        for step in range(3):
            index = step * 2 + pair
            rows = slice(8 * index, 8 * index + 8)
            stats = jnp.dot(table, spread_of(index), preferred_element_type=jnp.float32)[:8]
            peak = stats[:, :LANES]
            joint = jnp.maximum(peak, peak_ref[rows])
            near, far = jnp.exp(peak_ref[rows] - joint), jnp.exp(peak - joint)
            total = total_ref[rows] * near + stats[:, LANES:] * far
            summed = summed_ref[rows] * near + folded_ref[rows].astype(jnp.float32) * far
            attended = summed / total
            attended_ref[step, 2 * pair] = attended[:4].astype(jnp.bfloat16)
            attended_ref[step, 2 * pair + 1] = attended[4:].astype(jnp.bfloat16)


def merge(parts, folded, shape):
    return pl.pallas_call(
        merge_kernel,
        in_specs=[pl.BlockSpec(memory_space=pltpu.VMEM)] * 4,
        out_specs=pl.BlockSpec(memory_space=pltpu.VMEM),
        out_shape=jax.ShapeDtypeStruct(shape, jnp.bfloat16),
        compiler_params=pltpu.CompilerParams(vmem_limit_bytes=LIMIT),
        name="merge",
    )(*parts, folded)


def body(kv_cache, lengths, queries, new_kv, moving_slot, destination, block_index):
    halves = [NEAR, [HALF + member for member in NEAR]]
    planes = [PLANE, [8 + member for member in PLANE]]
    packed = pack(moving_slot, block_index, kv_cache, new_kv)
    pieces = lax.all_to_all(packed, "replica", 0, 0, tiled=True, axis_index_groups=halves)
    local = front(lengths, kv_cache, queries, packed)
    local, pieces = lax.optimization_barrier((local, pieces))
    chunks = lax.all_to_all(local, "tp", 0, 0, tiled=True, axis_index_groups=planes)
    ordered = order(destination, pieces)
    chunks, ordered = lax.optimization_barrier((chunks, ordered))
    tp_count = lax.axis_size("tp")
    groups = [[member * tp_count + t for member in MEMBERS[t // 8]] for t in range(tp_count)]
    delivered = lax.all_to_all(ordered, ("replica", "tp"), 0, 0, tiled=True, axis_index_groups=groups)
    half_sum = fold(chunks)
    folded = lax.ppermute(half_sum, "tp", [(i, i ^ 8) for i in range(16)])
    parts = own(chunks, queries, new_kv, half_sum)
    arrived, handed = unpack(destination, delivered, kv_cache.shape[-1])
    steps, req_dev, _, head_dim = queries.shape
    folded, arrived, handed = lax.optimization_barrier((folded, arrived, handed))
    attended = merge(parts, folded, (steps, req_dev, 4, head_dim))
    return (attended, arrived, handed)


def solution(mesh):
    placed = (
        P("replica", None, "tp", None),
        P("replica"),
        P(None, "replica", None, None),
        P(None, "replica", None, None),
        P("replica"),
        P(),
        P("replica"),
    )
    return jax.shard_map(
        body,
        mesh=mesh,
        in_specs=placed,
        out_specs=(
            P(None, "replica", "tp", None),
            P("replica", None, "tp", None),
            P("replica", None, None, None),
        ),
        check_vma=False,
    )
```
